32 devices in a mesh: grp: 2 (over y), frm: 4 (over z), head: 2 (over x), pos: 2 (over core).
Axes of the slice: x: 2, y: 2, z: 4, core: 2. Of those that a mesh axis runs over, the one named last changes fastest.
Arguments:
- queries: float32 [32, 128, 3072], P(('grp', 'frm'), 'pos', 'head'), parts along dimension 0, may hold values from -120 to 120
- key_states: float32 [32, 128, 3072], P(('grp', 'frm'), 'pos', 'head'), parts along dimension 0, may hold values from -4 to 4
- value_states: float32 [32, 128, 3072], P(('grp', 'frm'), 'pos', 'head'), parts along dimension 0, may hold values from -6 to 6
- windows: int32 [24], P('head'), may hold values from 1 to 2, as said below
- strides: int32 [24], P('head'), may hold values from 4 to 8, as said below
- cutoffs: int32 [24], P('head'), may hold values from 1 to 2, as said below
Outputs:
- blended: float32 [32, 128, 3072], P(('grp', 'frm'), 'pos', 'head'), parts along dimension 0
The draws below stay inside these ranges and needn't reach their ends.
There are 2 independent parts, one for each index of `grp`. The reference program is written for one: setup_inputs(seed, part) draws one part's arguments, and reference() takes and returns one part's arrays. A program takes and returns all parts, laid end to end along the dimension named above; an argument that names none is the same for every part. Nothing has to cross between parts.
Inputs may be any that keep to these rules, and one draw needn't show every extreme that they name: `windows`: some head has exactly 2. `strides`: each is 4 or 8, and both occur. `cutoffs`: some head has exactly 2.
All inputs are finite; a program needn't handle non-finite values.
Results may differ from the reference program's by a relative error of at most 0.0003.
Values sent between devices are 32-bit elements; how exact they have to be, the bound alone decides.
A program may use at most 128 MiB of HBM per device.

```python
import jax
import jax.numpy as jnp
from jax import lax

HEADS = 24
DH = 128
TOK_FRAME = 128
KSTRIDE = 4
FRAMES = 16
WMAX = 2
CMAX = 2


def shared_keys(key):
    split_one = jax.random.fold_in(jax.random.fold_in(key, 7), 0)
    key_values = jnp.clip(jax.random.normal(split_one, (FRAMES, TOK_FRAME, HEADS * DH), jnp.float32), -4.0, 4.0)
    return key_values


def draw_key_states(key, part):
    return shared_keys(key)


def draw_queries(key, part):
    query_key = jax.random.fold_in(key, 13)
    return 2.0 * jnp.clip(jax.random.normal(query_key, (FRAMES, TOK_FRAME, HEADS * DH), jnp.float32), -4.0, 4.0)


def draw_windows(key, part):
    split_one, split_two = jax.random.split(jax.random.fold_in(key, 21))
    drawn_widths = jax.random.randint(split_one, (HEADS,), 1, WMAX + 1)
    chosen = jax.random.randint(split_two, (), 0, HEADS)
    return drawn_widths.at[chosen].set(WMAX).astype(jnp.int32)


def draw_strides(key, part):
    split_one, split_two, split_three = jax.random.split(jax.random.fold_in(key, 31), 3)
    factors = jax.random.randint(split_one, (HEADS,), 1, 3)
    chosen = jax.random.randint(split_two, (), 0, HEADS)
    partner_head = (chosen + jax.random.randint(split_three, (), 1, HEADS)) % HEADS
    factors = factors.at[chosen].set(1).at[partner_head].set(2)
    return (factors * KSTRIDE).astype(jnp.int32)


def draw_cutoffs(key, part):
    split_one, split_two = jax.random.split(jax.random.fold_in(key, 41))
    drawn_cuts = jax.random.randint(split_one, (HEADS,), 1, CMAX + 1)
    chosen = jax.random.randint(split_two, (), 0, HEADS)
    return drawn_cuts.at[chosen].set(CMAX).astype(jnp.int32)


def block_levels(stream_key, dims, cuts, least, top_value):
    level = 1.0
    for axis_at, blocks in cuts:
        draws = jax.random.uniform(jax.random.fold_in(jax.random.fold_in(stream_key, 6), axis_at), (blocks,), jnp.float32, least / len(cuts), top_value / len(cuts))
        level = level * jnp.repeat(jnp.exp(draws), dims[axis_at] // blocks).reshape((-1,) + (1,) * (len(dims) - 1 - axis_at))
    return level


def noise(key, dims, spread, most, shards=(), kind=jnp.bfloat16):
    array = jax.random.normal(key, dims, jnp.float32) * spread
    if len(shards) > 0:
        array = block_levels(key, dims, shards, -0.22, 0.18) * array
    return jnp.clip(array, min=-most, max=most).astype(kind)


def setup_inputs(seed: int = 0, part: int = 0) -> dict:
    arg_keys = jax.random.split(jax.random.key(seed), 7)
    part_keys = jax.random.split(jax.random.fold_in(arg_keys[6], part), 7)
    return {
        "queries": draw_queries(jax.random.fold_in(jax.random.fold_in(arg_keys[6], part), 71), part),
        "key_states": draw_key_states(jax.random.fold_in(jax.random.fold_in(arg_keys[6], part), 71), part),
        "value_states": noise(part_keys[2], (FRAMES, TOK_FRAME, HEADS * DH), 1.0, 6.0, ((0, 4), (1, 2), (2, 2)), jnp.float32),
        "windows": draw_windows(jax.random.fold_in(arg_keys[6], 71), part),
        "strides": draw_strides(jax.random.fold_in(arg_keys[6], 71), part),
        "cutoffs": draw_cutoffs(jax.random.fold_in(arg_keys[6], 71), part),
    }


def masked_attend(query_part, key_part, value_part, allowed, score_scale):
    scores = jnp.einsum('phd,khd->hpk', query_part, key_part, precision=lax.Precision.HIGHEST) * score_scale
    highest = jnp.max(jnp.where(allowed[:, None, :], scores, -1e30), axis=2, keepdims=True)
    weights = jnp.where(allowed[:, None, :], jnp.exp(scores - highest), 0.0)
    row_total = jnp.sum(weights, axis=2, keepdims=True)
    return jnp.einsum('hpk,khd->phd', weights / row_total, value_part, precision=lax.Precision.HIGHEST)


def reference(queries, key_states, value_states, windows, strides, cutoffs):
    score_scale = DH ** -0.5
    query_grid = queries.reshape(FRAMES, TOK_FRAME, HEADS, DH)
    key_grid = key_states.reshape(FRAMES, TOK_FRAME, HEADS, DH)
    value_grid = value_states.reshape(FRAMES, TOK_FRAME, HEADS, DH)
    padding = ((WMAX, WMAX), (0, 0), (0, 0), (0, 0))
    padded_keys = jnp.pad(key_grid, padding)
    padded_values = jnp.pad(value_grid, padding)
    window_span = 2 * WMAX + 1
    key_offsets = jnp.repeat(jnp.arange(window_span, dtype=jnp.int32) - WMAX, TOK_FRAME)
    global_keys = key_grid[::KSTRIDE].reshape(-1, HEADS, DH)
    global_values = value_grid[::KSTRIDE].reshape(-1, HEADS, DH)
    global_frames = jnp.repeat(jnp.arange(0, FRAMES, KSTRIDE, dtype=jnp.int32), TOK_FRAME)
    global_allowed = (global_frames[None, :] % strides[:, None]) == 0

    def per_frame(frame_index):
        query_part = lax.dynamic_index_in_dim(query_grid, frame_index, 0, keepdims=False)
        near_keys = lax.dynamic_slice_in_dim(padded_keys, frame_index, window_span, 0).reshape(window_span * TOK_FRAME, HEADS, DH)
        near_values = lax.dynamic_slice_in_dim(padded_values, frame_index, window_span, 0).reshape(window_span * TOK_FRAME, HEADS, DH)
        near_frames = frame_index + key_offsets
        inside = (near_frames >= 0) & (near_frames < FRAMES)
        local_allowed = inside[None, :] & (jnp.abs(key_offsets)[None, :] <= windows[:, None])
        local_part = masked_attend(query_part, near_keys, near_values, local_allowed, score_scale)
        global_part = masked_attend(query_part, global_keys, global_values, global_allowed, score_scale)
        return local_part, global_part

    local, global_out = lax.map(per_frame, jnp.arange(FRAMES, dtype=jnp.int32))
    difference = global_out - local
    spectrum = jnp.fft.fft(difference, axis=0)
    frequency = jnp.arange(FRAMES, dtype=jnp.int32)
    distance_freq = jnp.minimum(frequency, FRAMES - frequency)
    low_keep = (distance_freq[:, None] <= cutoffs[None, :]).astype(difference.dtype)
    filtered = jnp.real(jnp.fft.ifft(spectrum * low_keep[:, None, :, None], axis=0))
    return (local + filtered).reshape(FRAMES, TOK_FRAME, HEADS * DH)
```

```python
import functools
import math

import jax
import jax.numpy as jnp
import numpy as np
from jax import lax
from jax.experimental import pallas as pl
from jax.experimental.pallas import tpu as pltpu
from jax.sharding import PartitionSpec as P

DH = 128
KSTRIDE = 4
MESH = pl.DeviceIdType.MESH
NEG = -1e30


def split_two(x):
    high = x.astype(jnp.bfloat16)
    low = (x - high.astype(jnp.float32)).astype(jnp.bfloat16)
    return high, low


def soft_rows(q_wide, keys, values, bias):
    rows = q_wide.shape[0]
    scores = lax.dot_general(
        q_wide, keys, (((1,), (1,)), ((), ())), preferred_element_type=jnp.float32
    )
    scores = scores + bias
    highest = jnp.max(scores, axis=1, keepdims=True)
    weights = jnp.exp(scores - highest)
    total = jnp.sum(weights, axis=1, keepdims=True)
    both = jnp.concatenate(split_two(weights), axis=0)
    wide = jnp.dot(both, values, preferred_element_type=jnp.float32)
    summed = (wide[:rows, :DH] + wide[:rows, DH:]) + (wide[rows:, :DH] + wide[rows:, DH:])
    return summed / total


def fill_split(key, value, keys_wide, values_wide, row, count):
    kh, kl = split_two(key)
    vh, vl = split_two(value)
    rows = pl.ds(row, count)
    keys_wide[rows, 0:DH] = kh
    keys_wide[rows, DH : 2 * DH] = kh
    keys_wide[rows, 2 * DH : 3 * DH] = kl
    keys_wide[rows, 3 * DH : 4 * DH] = kl
    values_wide[rows, 0:DH] = vh
    values_wide[rows, DH : 2 * DH] = vl


def kernel(
    sizes,
    win_ref, str_ref, cut_ref, basis_ref, q_ref, k_ref, v_ref, out_ref,
    ext, far, rowbuf, coef, rsum, lsum, ks, vs, kgs, vgs,
    x_own, x_send, x_recv, hr_send, hr_recv, hl_send, hl_recv, k_send, k_recv,
    cr_send, cr_recv, cl_send, cl_recv, o_own, o_send, o_recv,
):
    F, S, H, SHARED, Z, W, NC = sizes
    TOK = 2 * S
    z = lax.axis_index("frm")
    p = lax.axis_index("pos")
    other = 1 - p
    has_right = z < Z - 1
    has_left = z > 0
    right = jnp.minimum(z + 1, Z - 1)
    left = jnp.maximum(z - 1, 0)
    to_right, to_left, to_other = {"frm": right}, {"frm": left}, {"pos": other}

    def remote(src, dst, send, recv, to):
        return pltpu.make_async_remote_copy(
            src_ref=src, dst_ref=dst, send_sem=send, recv_sem=recv, device_id=to, device_id_type=MESH
        )

    def col(half, j):
        return pl.ds(pl.multiple_of((half * (H - SHARED) + j) * DH, DH), DH)

    my_rows = pl.ds(pl.multiple_of(p * S, S), S)
    other_rows = pl.ds(pl.multiple_of(other * S, S), S)

    def place(which, j, rows):
        if which == 0:
            return rowbuf.at[j, :, rows]
        return ext.at[j, which - 1, pl.ds(W, F), rows]

    sources = (q_ref, k_ref, v_ref)

    def own_copy(which, j):
        return pltpu.make_async_copy(
            sources[which].at[:, :, col(p, j)], place(which, j, my_rows), x_own.at[which, j]
        )

    def swap(which, j):
        return remote(
            sources[which].at[:, :, col(other, j)], place(which, j, my_rows),
            x_send.at[which, j], x_recv.at[which, j], to_other,
        )

    def halo_right(j):
        return remote(
            ext.at[j, :, pl.ds(F, W)], ext.at[j, :, pl.ds(0, W)], hr_send.at[j], hr_recv.at[j], to_right
        )

    def halo_left(j):
        return remote(
            ext.at[j, :, pl.ds(W, W)], ext.at[j, :, pl.ds(F + W, W)], hl_send.at[j], hl_recv.at[j], to_left
        )

    def key_copy(src, j, g, to):
        return remote(src, far.at[j, :, g], k_send.at[j, g], k_recv.at[j, g], to)

    def key_here(j, g, to):
        return key_copy(far.at[j, :, g], j, g, to)

    def sum_right(j):
        return remote(rsum.at[j], rsum.at[j], cr_send.at[j], cr_recv.at[j], to_right)

    def sum_left(j):
        return remote(lsum.at[j], lsum.at[j], cl_send.at[j], cl_recv.at[j], to_left)

    def out_own(j):
        return pltpu.make_async_copy(
            rowbuf.at[j, :, my_rows], out_ref.at[:, :, col(p, j)], o_own.at[j]
        )

    def out_other(j):
        return remote(
            rowbuf.at[j, :, other_rows], out_ref.at[:, :, col(p, j)], o_send.at[j], o_recv.at[j], to_other
        )

    barrier = pltpu.get_barrier_semaphore()
    pl.semaphore_signal(barrier, inc=1, device_id=to_other, device_id_type=MESH)

    @pl.when(has_right)
    def _():
        pl.semaphore_signal(barrier, inc=1, device_id=to_right, device_id_type=MESH)

    @pl.when(has_left)
    def _():
        pl.semaphore_signal(barrier, inc=1, device_id=to_left, device_id_type=MESH)

    pl.semaphore_wait(barrier, 1 + has_right.astype(jnp.int32) + has_left.astype(jnp.int32))

    def alone(half, j):
        if SHARED == 0:
            return j >= 0
        return jnp.where(half == 0, j < H - SHARED, j >= SHARED)

    order = (1, 2, 0)

    @pl.loop(0, H)
    def _(j):
        for which in order:
            swap(which, j).start()
            own_copy(which, j).start()

    def zero_halo(first):
        @pl.loop(0, H)
        def _(j):
            ext[j, :, first : first + W] = jnp.zeros((2, W, TOK, DH), jnp.float32)

    @pl.when(jnp.logical_not(has_left))
    def _():
        zero_halo(0)

    @pl.when(jnp.logical_not(has_right))
    def _():
        zero_halo(F + W)

    def arrive(which, j):
        own_copy(which, j).wait()
        swap(which, j).wait_recv()

    def compute(j):
        head = p * (H - SHARED) + j
        window = win_ref[head]
        stride = str_ref[head]
        cutoff = cut_ref[head]
        for e in range(F + 2 * W):
            fill_split(ext[j, 0, e], ext[j, 1, e], ks, vs, e * TOK, TOK)
        far[j, :, z] = ext[j, :, W]

        @pl.when(has_right)
        def _():
            far[j, :, z + 1] = ext[j, :, F + W]

        for g in range(Z):
            fill_split(far[j, 0, g], far[j, 1, g], kgs, vgs, g * TOK, TOK)

        def bias_row(flags):
            return jnp.concatenate(
                [jnp.full((1, TOK), jnp.where(ok, 0.0, NEG), jnp.float32) for ok in flags], axis=1
            )

        far_bias = bias_row([((g * KSTRIDE) & (stride - 1)) == 0 for g in range(Z)])
        diffs = []
        for i in range(F):
            qh, ql = split_two(rowbuf[j, i] * (DH**-0.5))
            q_wide = jnp.concatenate([qh, ql, qh, ql], axis=1)
            flags = []
            for off in range(-W, W + 1):
                frame = z * F + i + off
                flags.append((abs(off) <= window) & (frame >= 0) & (frame < Z * F))
            near_rows = pl.ds(i * TOK, (2 * W + 1) * TOK)
            local = soft_rows(q_wide, ks[near_rows], vs[near_rows], bias_row(flags))
            wide = soft_rows(q_wide, kgs[...], vgs[...], far_bias)
            rowbuf[j, i] = local
            diffs.append(wide - local)
        for c in range(NC):
            acc = diffs[0] * basis_ref[(z * F) * NC + c]
            for i in range(1, F):
                acc = acc + diffs[i] * basis_ref[(z * F + i) * NC + c]
            keep = jnp.where((c + 1) // 2 <= cutoff, 1.0, 0.0)
            coef[j, c] = acc * keep

    def finish(j):
        totals = [(rsum[j, c] - coef[j, c]) + lsum[j, c] for c in range(NC)]
        for i in range(F):
            acc = rowbuf[j, i]
            for c in range(NC):
                acc = acc + totals[c] * basis_ref[(z * F + i) * NC + c]
            rowbuf[j, i] = acc
        out_own(j).start()

        @pl.when(alone(p, j))
        def _():
            out_other(j).start()

    reach = Z - 1
    last = jnp.maximum(z, Z - 1 - z)

    def valid(j):
        return (j >= 0) & (j < H)

    @pl.loop(0, H + 2 * reach)
    def _(t):
        @pl.when(t < H)
        def _():
            arrive(1, t)
            arrive(2, t)

            @pl.when(has_right)
            def _():
                key_copy(ext.at[t, :, W], t, z, to_right).start()
                halo_right(t).start()

            @pl.when(has_left)
            def _():
                halo_left(t).start()

        @pl.when(valid(t - 1) & has_right)
        def _():
            halo_left(t - 1).wait_recv()

            @pl.when(has_left)
            def _():
                key_copy(ext.at[t - 1, :, F + W], t - 1, z + 1, to_left).start()

        for d in range(1, Z):
            @pl.when(valid(t - d) & (z - d >= 0))
            def _():
                key_here(t - d, z - d, to_right).wait_recv()

                @pl.when(has_right)
                def _():
                    key_here(t - d, z - d, to_right).start()

        for d in range(2, Z):
            @pl.when(valid(t - d) & (z + d < Z))
            def _():
                key_here(t - d, z + d, to_left).wait_recv()

                @pl.when(has_left)
                def _():
                    key_here(t - d, z + d, to_left).start()

        now = t - reach

        @pl.when(valid(now))
        def _():
            arrive(0, now)

            @pl.when(has_left)
            def _():
                halo_right(now).wait_recv()

            compute(now)

        jr = now - z

        @pl.when(valid(jr))
        def _():
            @pl.when(has_left)
            def _():
                sum_right(jr).wait_recv()
                rsum[jr] = rsum[jr] + coef[jr]

            @pl.when(jnp.logical_not(has_left))
            def _():
                rsum[jr] = coef[jr]

            @pl.when(has_right)
            def _():
                sum_right(jr).start()

        jl = now - (Z - 1 - z)

        @pl.when(valid(jl))
        def _():
            @pl.when(has_right)
            def _():
                sum_left(jl).wait_recv()
                lsum[jl] = lsum[jl] + coef[jl]

            @pl.when(jnp.logical_not(has_right))
            def _():
                lsum[jl] = coef[jl]

            @pl.when(has_left)
            def _():
                sum_left(jl).start()

        jf = now - last

        @pl.when(valid(jf))
        def _():
            finish(jf)

    @pl.loop(0, H)
    def _(j):
        for which in range(3):
            swap(which, j).wait_send()

        @pl.when(has_right)
        def _():
            halo_right(j).wait_send()
            sum_right(j).wait_send()
            key_copy(ext.at[j, :, W], j, z, to_right).wait_send()

        @pl.when(has_left)
        def _():
            halo_left(j).wait_send()
            sum_left(j).wait_send()

        @pl.when(has_left & has_right)
        def _():
            key_copy(ext.at[j, :, F + W], j, z + 1, to_left).wait_send()

        for d in range(1, Z):
            @pl.when((z - d >= 0) & has_right)
            def _():
                key_here(j, z - d, to_right).wait_send()

        for d in range(2, Z):
            @pl.when((z + d < Z) & has_left)
            def _():
                key_here(j, z + d, to_left).wait_send()

        out_own(j).wait()

        @pl.when(alone(p, j))
        def _():
            out_other(j).wait_send()

        @pl.when(alone(other, j))
        def _():
            out_other(j).wait_recv()


def basis_table(total_frames, top):
    frames = np.arange(total_frames)
    columns = [np.full(total_frames, math.sqrt(1.0 / total_frames))]
    for k in range(1, top + 1):
        phase = 2.0 * math.pi * ((k * frames) % total_frames) / total_frames
        columns.append(math.sqrt(2.0 / total_frames) * np.cos(phase))
        columns.append(math.sqrt(2.0 / total_frames) * np.sin(phase))
    return np.stack(columns, axis=1).astype(np.float32)


def shards(queries, key_states, value_states, windows, strides, cutoffs):
    F, S, channels = queries.shape
    Z = lax.axis_size("frm")
    heads = channels // DH
    H = (heads + 1) // 2
    SHARED = 2 * H - heads
    W = F // 2
    assert lax.axis_size("pos") == 2 and F == KSTRIDE
    basis = basis_table(F * Z, F * Z // 8)
    NC = basis.shape[1]
    TOK = 2 * S
    dma = pltpu.SemaphoreType.DMA
    f32, bf16 = jnp.float32, jnp.bfloat16
    return pl.pallas_call(
        functools.partial(kernel, (F, S, H, SHARED, Z, W, NC)),
        out_shape=jax.ShapeDtypeStruct(queries.shape, f32),
        in_specs=[pl.BlockSpec(memory_space=pltpu.SMEM)] * 4 + [pl.BlockSpec(memory_space=pl.ANY)] * 3,
        out_specs=pl.BlockSpec(memory_space=pl.ANY),
        scratch_shapes=[
            pltpu.VMEM((H, 2, F + 2 * W, TOK, DH), f32),
            pltpu.VMEM((H, 2, Z, TOK, DH), f32),
            pltpu.VMEM((H, F, TOK, DH), f32),
            pltpu.VMEM((H, NC, TOK, DH), f32),
            pltpu.VMEM((H, NC, TOK, DH), f32),
            pltpu.VMEM((H, NC, TOK, DH), f32),
            pltpu.VMEM(((F + 2 * W) * TOK, 4 * DH), bf16),
            pltpu.VMEM(((F + 2 * W) * TOK, 2 * DH), bf16),
            pltpu.VMEM((Z * TOK, 4 * DH), bf16),
            pltpu.VMEM((Z * TOK, 2 * DH), bf16),
            dma((3, H)), dma((3, H)), dma((3, H)),
            dma((H,)), dma((H,)), dma((H,)), dma((H,)),
            dma((H, Z)), dma((H, Z)),
            dma((H,)), dma((H,)), dma((H,)), dma((H,)),
            dma((H,)), dma((H,)), dma((H,)),
        ],
        compiler_params=pltpu.CompilerParams(
            collective_id=0, has_side_effects=True, vmem_limit_bytes=60 * 1024 * 1024
        ),
    )(windows, strides, cutoffs, jnp.asarray(basis.reshape(-1)), queries, key_states, value_states)


def solution(mesh):
    in_specs = (
        P(("grp", "frm"), "pos", "head"),
        P(("grp", "frm"), "pos", "head"),
        P(("grp", "frm"), "pos", "head"),
        P("head"),
        P("head"),
        P("head"),
    )
    out_specs = P(("grp", "frm"), "pos", "head")
    return jax.shard_map(shards, mesh=mesh, in_specs=in_specs, out_specs=out_specs, check_vma=False)
```

```python
import functools
import math

import jax
import jax.numpy as jnp
import numpy as np
from jax import lax
from jax.experimental import pallas as pl
from jax.experimental.pallas import tpu as pltpu
from jax.sharding import PartitionSpec as P

DH = 128
KSTRIDE = 4
MESH = pl.DeviceIdType.MESH
NEG = -1e30


def split_two(x):
    high = x.astype(jnp.bfloat16)
    low = (x - high.astype(jnp.float32)).astype(jnp.bfloat16)
    return high, low


def soft_rows(q_wide, keys, values, bias):
    rows = q_wide.shape[0]
    scores = lax.dot_general(
        q_wide, keys, (((1,), (1,)), ((), ())), preferred_element_type=jnp.float32
    )
    scores = scores + bias
    highest = jnp.max(scores, axis=1, keepdims=True)
    weights = jnp.exp(scores - highest)
    total = jnp.sum(weights, axis=1, keepdims=True)
    both = jnp.concatenate(split_two(weights), axis=0)
    wide = jnp.dot(both, values, preferred_element_type=jnp.float32)
    summed = (wide[:rows, :DH] + wide[:rows, DH:]) + (wide[rows:, :DH] + wide[rows:, DH:])
    return summed / total


def fill_split(key, value, keys_wide, values_wide, row, count):
    kh, kl = split_two(key)
    vh, vl = split_two(value)
    rows = pl.ds(row, count)
    keys_wide[rows, 0:DH] = kh
    keys_wide[rows, DH : 2 * DH] = kh
    keys_wide[rows, 2 * DH : 3 * DH] = kl
    keys_wide[rows, 3 * DH : 4 * DH] = kl
    values_wide[rows, 0:DH] = vh
    values_wide[rows, DH : 2 * DH] = vl


def kernel(
    sizes,
    win_ref, str_ref, cut_ref, basis_ref, q_ref, k_ref, v_ref, out_ref,
    ext, far, rowbuf, coef, rsum, lsum, edge_r, edge_l, dbuf, ks, vs, kgs, vgs,
    x_own, x_send, x_recv, hr_send, hr_recv, hl_send, hl_recv, k_send, k_recv,
    cr_send, cr_recv, cl_send, cl_recv, q_send, q_recv, o_own, o_send, o_recv,
):
    F, S, H, SHARED, Z, W, NC = sizes
    TOK = 2 * S
    z = lax.axis_index("frm")
    p = lax.axis_index("pos")
    other = 1 - p
    has_right = z < Z - 1
    has_left = z > 0
    right = jnp.minimum(z + 1, Z - 1)
    left = jnp.maximum(z - 1, 0)
    is_first = z == 0
    is_last = z == Z - 1
    is_helper = z == Z - 2
    keys_right = z < Z - 2
    to_right, to_left, to_other = {"frm": right}, {"frm": left}, {"pos": other}

    def remote(src, dst, send, recv, to):
        return pltpu.make_async_remote_copy(
            src_ref=src, dst_ref=dst, send_sem=send, recv_sem=recv, device_id=to, device_id_type=MESH
        )

    def col(half, j):
        return pl.ds(pl.multiple_of((half * (H - SHARED) + j) * DH, DH), DH)

    my_rows = pl.ds(pl.multiple_of(p * S, S), S)
    other_rows = pl.ds(pl.multiple_of(other * S, S), S)

    def place(which, j, rows):
        if which == 0:
            return rowbuf.at[j, pl.ds(0, F), rows]
        return ext.at[j, which - 1, pl.ds(W, F), rows]

    sources = (q_ref, k_ref, v_ref)

    def own_copy(which, j):
        return pltpu.make_async_copy(
            sources[which].at[:, :, col(p, j)], place(which, j, my_rows), x_own.at[which, j]
        )

    def swap(which, j):
        return remote(
            sources[which].at[:, :, col(other, j)], place(which, j, my_rows),
            x_send.at[which, j], x_recv.at[which, j], to_other,
        )

    def halo_right(j):
        return remote(
            ext.at[j, :, pl.ds(F, W)], ext.at[j, :, pl.ds(0, W)], hr_send.at[j], hr_recv.at[j], to_right
        )

    def halo_left(j):
        return remote(
            ext.at[j, :, pl.ds(W, W)], ext.at[j, :, pl.ds(F + W, W)], hl_send.at[j], hl_recv.at[j], to_left
        )

    def key_copy(src, j, g, to):
        return remote(src, far.at[j, :, g], k_send.at[j, g], k_recv.at[j, g], to)

    def key_here(j, g, to):
        return key_copy(far.at[j, :, g], j, g, to)

    def sum_right_full(j):
        return remote(rsum.at[j], rsum.at[j], cr_send.at[j], cr_recv.at[j], to_right)

    def sum_right_first(j):
        part = rsum.at[j, pl.ds(0, F)]
        return remote(part, part, cr_send.at[j], cr_recv.at[j], to_right)

    def sum_right_last(j):
        return remote(edge_r.at[j], rsum.at[j, pl.ds(0, F)], cr_send.at[j], cr_recv.at[j], to_right)

    def sum_left_full(j):
        return remote(lsum.at[j], lsum.at[j], cl_send.at[j], cl_recv.at[j], to_left)

    def sum_left_first(j):
        part = lsum.at[j, pl.ds(0, F)]
        return remote(part, part, cl_send.at[j], cl_recv.at[j], to_left)

    def sum_left_last(j):
        return remote(edge_l.at[j], lsum.at[j, pl.ds(0, F)], cl_send.at[j], cl_recv.at[j], to_left)

    def query_left(j):
        return remote(
            rowbuf.at[j, pl.ds(0, F)], rowbuf.at[j, pl.ds(F, F)], q_send.at[j], q_recv.at[j], to_left
        )

    def out_own(j):
        return pltpu.make_async_copy(
            rowbuf.at[j, pl.ds(0, F), my_rows], out_ref.at[:, :, col(p, j)], o_own.at[j]
        )

    def out_other(j):
        return remote(
            rowbuf.at[j, pl.ds(0, F), other_rows], out_ref.at[:, :, col(p, j)], o_send.at[j], o_recv.at[j], to_other
        )

    barrier = pltpu.get_barrier_semaphore()
    pl.semaphore_signal(barrier, inc=1, device_id=to_other, device_id_type=MESH)

    @pl.when(has_right)
    def _():
        pl.semaphore_signal(barrier, inc=1, device_id=to_right, device_id_type=MESH)

    @pl.when(has_left)
    def _():
        pl.semaphore_signal(barrier, inc=1, device_id=to_left, device_id_type=MESH)

    pl.semaphore_wait(barrier, 1 + has_right.astype(jnp.int32) + has_left.astype(jnp.int32))

    def alone(half, j):
        if SHARED == 0:
            return j >= 0
        return jnp.where(half == 0, j < H - SHARED, j >= SHARED)

    order = (1, 2, 0)

    @pl.loop(0, H)
    def _(j):
        for which in order:
            swap(which, j).start()
            own_copy(which, j).start()

    def zero_halo(first):
        @pl.loop(0, H)
        def _(j):
            ext[j, :, first : first + W] = jnp.zeros((2, W, TOK, DH), jnp.float32)

    @pl.when(jnp.logical_not(has_left))
    def _():
        zero_halo(0)

    @pl.when(jnp.logical_not(has_right))
    def _():
        zero_halo(F + W)

    def arrive(which, j):
        own_copy(which, j).wait()
        swap(which, j).wait_recv()

    def compute(j):
        head = p * (H - SHARED) + j
        window = win_ref[head]
        stride = str_ref[head]
        for e in range(F + 2 * W):
            fill_split(ext[j, 0, e], ext[j, 1, e], ks, vs, e * TOK, TOK)

        def bias_row(flags):
            return jnp.concatenate(
                [jnp.full((1, TOK), jnp.where(ok, 0.0, NEG), jnp.float32) for ok in flags], axis=1
            )

        def wide_query(i):
            qh, ql = split_two(rowbuf[j, i] * (DH**-0.5))
            return jnp.concatenate([qh, ql, qh, ql], axis=1)

        @pl.when(jnp.logical_not(is_last))
        def _():
            far[j, :, z] = ext[j, :, W]
            far[j, :, z + 1] = ext[j, :, F + W]
            for g in range(Z):
                fill_split(far[j, 0, g], far[j, 1, g], kgs, vgs, g * TOK, TOK)
            far_bias = bias_row([((g * KSTRIDE) & (stride - 1)) == 0 for g in range(Z)])

            @pl.loop(0, jnp.where(is_helper, 2 * F, F))
            def _(i):
                dbuf[i] = soft_rows(wide_query(i), kgs[...], vgs[...], far_bias)

        @pl.when(is_last)
        def _():
            dbuf[0:F] = jnp.zeros((F, TOK, DH), jnp.float32)

        for i in range(F):
            flags = []
            for off in range(-W, W + 1):
                frame = z * F + i + off
                flags.append((abs(off) <= window) & (frame >= 0) & (frame < Z * F))
            near_rows = pl.ds(i * TOK, (2 * W + 1) * TOK)
            local = soft_rows(wide_query(i), ks[near_rows], vs[near_rows], bias_row(flags))
            rowbuf[j, i] = local
            dbuf[i] = dbuf[i] - local
        for c in range(NC):
            coef[j, c] = keep_of(j, c) * project([dbuf[i] for i in range(F)], z, c)

        @pl.when(is_helper)
        def _():
            for c in range(NC):
                more = project([dbuf[F + i] for i in range(F)], Z - 1, c)
                coef[j, c] = coef[j, c] + keep_of(j, c) * more

        @pl.when(is_first)
        def _():
            rsum[j, 0:F] = dbuf[0:F]

        @pl.when(is_last)
        def _():
            lsum[j, 0:F] = dbuf[0:F]

    def keep_of(j, c):
        return jnp.where((c + 1) // 2 <= cut_ref[p * (H - SHARED) + j], 1.0, 0.0)

    def project(frames, at, c):
        acc = frames[0] * basis_ref[at * F * NC + c]
        for i in range(1, F):
            acc = acc + frames[i] * basis_ref[(at * F + i) * NC + c]
        return acc

    def expand(start, totals, at, i):
        for c in range(NC):
            part = totals[c] * basis_ref[(at * F + i) * NC + c]
            start = part if start is None else start + part
        return start

    def finish(j):
        def ends(received):
            totals = [coef[j, c] for c in range(NC)]
            for i in range(F):
                rowbuf[j, i] = expand(rowbuf[j, i] + received[j, i], totals, z, i)

        @pl.when(is_first)
        def _():
            ends(lsum)

        @pl.when(is_last)
        def _():
            ends(rsum)

        @pl.when(has_left & has_right)
        def _():
            totals = [(rsum[j, c] - coef[j, c]) + lsum[j, c] for c in range(NC)]
            for i in range(F):
                rowbuf[j, i] = expand(rowbuf[j, i], totals, z, i)

        out_own(j).start()

        @pl.when(alone(p, j))
        def _():
            out_other(j).start()

    def add_raw(sums, j, at):
        raw = [sums[j, i] for i in range(F)]
        for c in range(NC):
            sums[j, c] = coef[j, c] + keep_of(j, c) * project(raw, at, c)

    def fill_edge(edge, sums, j, at):
        totals = [sums[j, c] for c in range(NC)]
        for i in range(F):
            edge[j, i] = expand(None, totals, at, i)

    delay = jnp.where(is_last, 1, jnp.maximum(z, Z - 1 - z))
    right_delay = Z - 1 + z
    left_delay = jnp.where(is_last, 1, 2 * Z - 4 - z)
    last_delay = jnp.maximum(right_delay, left_delay)
    from_first = z == 1
    middle_in_right = (z > 1) & (z < Z - 1)
    middle_in_left = (z > 0) & (z < Z - 2)
    middle_out_right = (z > 0) & (z < Z - 2)
    middle_out_left = (z > 1) & (z < Z - 1)

    def valid(j):
        return (j >= 0) & (j < H)

    @pl.loop(0, H + 2 * Z - 2)
    def _(t):
        @pl.when(t < H)
        def _():
            arrive(1, t)
            arrive(2, t)

            @pl.when(keys_right)
            def _():
                key_copy(ext.at[t, :, W], t, z, to_right).start()

            @pl.when(has_right)
            def _():
                halo_right(t).start()

            @pl.when(has_left)
            def _():
                halo_left(t).start()

            arrive(0, t)

            @pl.when(is_last)
            def _():
                query_left(t).start()

        @pl.when(valid(t - 1) & has_right)
        def _():
            halo_left(t - 1).wait_recv()

            @pl.when(has_left)
            def _():
                key_copy(ext.at[t - 1, :, F + W], t - 1, z + 1, to_left).start()

        for d in range(1, Z - 1):
            @pl.when(valid(t - d) & (z - d >= 0) & jnp.logical_not(is_last))
            def _():
                key_here(t - d, z - d, to_right).wait_recv()

                @pl.when(keys_right)
                def _():
                    key_here(t - d, z - d, to_right).start()

        for d in range(2, Z):
            @pl.when(valid(t - d) & (z + d < Z))
            def _():
                key_here(t - d, z + d, to_left).wait_recv()

                @pl.when(has_left)
                def _():
                    key_here(t - d, z + d, to_left).start()

        now = t - delay

        @pl.when(valid(now))
        def _():
            @pl.when(has_left)
            def _():
                halo_right(now).wait_recv()

            @pl.when(is_helper)
            def _():
                query_left(now).wait_recv()

            @pl.when(is_last)
            def _():
                query_left(now).wait_send()

            compute(now)

        jr = t - right_delay

        @pl.when(valid(jr))
        def _():
            @pl.when(is_first)
            def _():
                sum_right_first(jr).start()

            @pl.when(from_first)
            def _():
                sum_right_first(jr).wait_recv()
                add_raw(rsum, jr, 0)

            @pl.when(middle_in_right)
            def _():
                sum_right_full(jr).wait_recv()
                rsum[jr] = rsum[jr] + coef[jr]

            @pl.when(is_last)
            def _():
                sum_right_last(jr).wait_recv()

            @pl.when(middle_out_right)
            def _():
                sum_right_full(jr).start()

            @pl.when(is_helper)
            def _():
                fill_edge(edge_r, rsum, jr, Z - 1)
                sum_right_last(jr).start()

        jl = t - left_delay

        @pl.when(valid(jl))
        def _():
            @pl.when(is_last)
            def _():
                sum_left_first(jl).start()

            @pl.when(is_helper)
            def _():
                sum_left_first(jl).wait_recv()
                add_raw(lsum, jl, Z - 1)

            @pl.when(middle_in_left)
            def _():
                sum_left_full(jl).wait_recv()
                lsum[jl] = lsum[jl] + coef[jl]

            @pl.when(is_first)
            def _():
                sum_left_last(jl).wait_recv()

            @pl.when(middle_out_left)
            def _():
                sum_left_full(jl).start()

            @pl.when(from_first)
            def _():
                fill_edge(edge_l, lsum, jl, 0)
                sum_left_last(jl).start()

        jf = t - last_delay

        @pl.when(valid(jf))
        def _():
            finish(jf)

    @pl.loop(0, H)
    def _(j):
        for which in range(3):
            swap(which, j).wait_send()

        @pl.when(keys_right)
        def _():
            key_copy(ext.at[j, :, W], j, z, to_right).wait_send()

        @pl.when(has_right)
        def _():
            halo_right(j).wait_send()

        @pl.when(has_left)
        def _():
            halo_left(j).wait_send()

        @pl.when(is_first)
        def _():
            sum_right_first(j).wait_send()

        @pl.when(middle_out_right)
        def _():
            sum_right_full(j).wait_send()

        @pl.when(is_helper)
        def _():
            sum_right_last(j).wait_send()

        @pl.when(is_last)
        def _():
            sum_left_first(j).wait_send()

        @pl.when(middle_out_left)
        def _():
            sum_left_full(j).wait_send()

        @pl.when(from_first)
        def _():
            sum_left_last(j).wait_send()

        @pl.when(has_left & has_right)
        def _():
            key_copy(ext.at[j, :, F + W], j, z + 1, to_left).wait_send()

        for d in range(1, Z - 1):
            @pl.when((z - d >= 0) & keys_right)
            def _():
                key_here(j, z - d, to_right).wait_send()

        for d in range(2, Z):
            @pl.when((z + d < Z) & has_left)
            def _():
                key_here(j, z + d, to_left).wait_send()

        out_own(j).wait()

        @pl.when(alone(p, j))
        def _():
            out_other(j).wait_send()

        @pl.when(alone(other, j))
        def _():
            out_other(j).wait_recv()


def basis_table(total_frames, top):
    frames = np.arange(total_frames)
    columns = [np.full(total_frames, math.sqrt(1.0 / total_frames))]
    for k in range(1, top + 1):
        phase = 2.0 * math.pi * ((k * frames) % total_frames) / total_frames
        columns.append(math.sqrt(2.0 / total_frames) * np.cos(phase))
        columns.append(math.sqrt(2.0 / total_frames) * np.sin(phase))
    return np.stack(columns, axis=1).astype(np.float32)


def shards(queries, key_states, value_states, windows, strides, cutoffs):
    F, S, channels = queries.shape
    Z = lax.axis_size("frm")
    heads = channels // DH
    H = (heads + 1) // 2
    SHARED = 2 * H - heads
    W = F // 2
    basis = basis_table(F * Z, F * Z // 8)
    NC = basis.shape[1]
    assert lax.axis_size("pos") == 2 and F == KSTRIDE and Z >= 3 and NC >= F
    TOK = 2 * S
    dma = pltpu.SemaphoreType.DMA
    f32, bf16 = jnp.float32, jnp.bfloat16
    return pl.pallas_call(
        functools.partial(kernel, (F, S, H, SHARED, Z, W, NC)),
        out_shape=jax.ShapeDtypeStruct(queries.shape, f32),
        in_specs=[pl.BlockSpec(memory_space=pltpu.SMEM)] * 4 + [pl.BlockSpec(memory_space=pl.ANY)] * 3,
        out_specs=pl.BlockSpec(memory_space=pl.ANY),
        scratch_shapes=[
            pltpu.VMEM((H, 2, F + 2 * W, TOK, DH), f32),
            pltpu.VMEM((H, 2, Z, TOK, DH), f32),
            pltpu.VMEM((H, 2 * F, TOK, DH), f32),
            pltpu.VMEM((H, NC, TOK, DH), f32),
            pltpu.VMEM((H, NC, TOK, DH), f32),
            pltpu.VMEM((H, NC, TOK, DH), f32),
            pltpu.VMEM((H, F, TOK, DH), f32),
            pltpu.VMEM((H, F, TOK, DH), f32),
            pltpu.VMEM((2 * F, TOK, DH), f32),
            pltpu.VMEM(((F + 2 * W) * TOK, 4 * DH), bf16),
            pltpu.VMEM(((F + 2 * W) * TOK, 2 * DH), bf16),
            pltpu.VMEM((Z * TOK, 4 * DH), bf16),
            pltpu.VMEM((Z * TOK, 2 * DH), bf16),
            dma((3, H)), dma((3, H)), dma((3, H)),
            dma((H,)), dma((H,)), dma((H,)), dma((H,)),
            dma((H, Z)), dma((H, Z)),
            dma((H,)), dma((H,)), dma((H,)), dma((H,)),
            dma((H,)), dma((H,)), dma((H,)), dma((H,)), dma((H,)),
        ],
        compiler_params=pltpu.CompilerParams(
            collective_id=0, has_side_effects=True, vmem_limit_bytes=60 * 1024 * 1024
        ),
    )(windows, strides, cutoffs, jnp.asarray(basis.reshape(-1)), queries, key_states, value_states)


def solution(mesh):
    in_specs = (
        P(("grp", "frm"), "pos", "head"),
        P(("grp", "frm"), "pos", "head"),
        P(("grp", "frm"), "pos", "head"),
        P("head"),
        P("head"),
        P("head"),
    )
    out_specs = P(("grp", "frm"), "pos", "head")
    return jax.shard_map(shards, mesh=mesh, in_specs=in_specs, out_specs=out_specs, check_vma=False)
```

```python
import functools
import math

import jax
import jax.numpy as jnp
import numpy as np
from jax import lax
from jax.experimental import pallas as pl
from jax.experimental.pallas import tpu as pltpu
from jax.sharding import PartitionSpec as P

DH = 128
KSTRIDE = 4
MESH = pl.DeviceIdType.MESH
NEG = -1e30


def split_two(x):
    high = x.astype(jnp.bfloat16)
    low = (x - high.astype(jnp.float32)).astype(jnp.bfloat16)
    return high, low


def soft_rows(q_wide, keys, values, bias):
    rows = q_wide.shape[0]
    scores = lax.dot_general(
        q_wide, keys, (((1,), (1,)), ((), ())), preferred_element_type=jnp.float32
    )
    scores = scores + bias
    highest = jnp.max(scores, axis=1, keepdims=True)
    weights = jnp.exp(scores - highest)
    total = jnp.sum(weights, axis=1, keepdims=True)
    both = jnp.concatenate(split_two(weights), axis=0)
    wide = jnp.dot(both, values, preferred_element_type=jnp.float32)
    summed = (wide[:rows, :DH] + wide[:rows, DH:]) + (wide[rows:, :DH] + wide[rows:, DH:])
    return summed / total


def fill_split(key, value, keys_wide, values_wide, row, count):
    kh, kl = split_two(key)
    vh, vl = split_two(value)
    rows = pl.ds(row, count)
    keys_wide[rows, 0:DH] = kh
    keys_wide[rows, DH : 2 * DH] = kh
    keys_wide[rows, 2 * DH : 3 * DH] = kl
    keys_wide[rows, 3 * DH : 4 * DH] = kl
    values_wide[rows, 0:DH] = vh
    values_wide[rows, DH : 2 * DH] = vl


def kernel(
    sizes,
    win_ref, str_ref, cut_ref, basis_ref, q_ref, k_ref, v_ref, out_ref,
    ext, far, rowbuf, coef, rsum, lsum, edge_r, edge_l, dbuf, ks, vs, kgs, vgs,
    x_own, x_send, x_recv, hr_send, hr_recv, hl_send, hl_recv, k_send, k_recv,
    cr_send, cr_recv, cl_send, cl_recv, q_send, q_recv, o_own, o_send, o_recv,
):
    F, S, H, SHARED, Z, W, NC = sizes
    TOK = 2 * S
    z = lax.axis_index("frm")
    p = lax.axis_index("pos")
    other = 1 - p
    has_right = z < Z - 1
    has_left = z > 0
    right = jnp.minimum(z + 1, Z - 1)
    left = jnp.maximum(z - 1, 0)
    is_first = z == 0
    is_last = z == Z - 1
    is_helper = z == Z - 2
    keys_right = z < Z - 2
    to_right, to_left, to_other = {"frm": right}, {"frm": left}, {"pos": other}

    def remote(src, dst, send, recv, to):
        return pltpu.make_async_remote_copy(
            src_ref=src, dst_ref=dst, send_sem=send, recv_sem=recv, device_id=to, device_id_type=MESH
        )

    def col(half, j):
        return pl.ds(pl.multiple_of((half * (H - SHARED) + j) * DH, DH), DH)

    my_rows = pl.ds(pl.multiple_of(p * S, S), S)
    other_rows = pl.ds(pl.multiple_of(other * S, S), S)

    def place(which, j, rows):
        if which == 0:
            return rowbuf.at[j, pl.ds(0, F), rows]
        return ext.at[j, which - 1, pl.ds(W, F), rows]

    sources = (q_ref, k_ref, v_ref)

    def own_copy(which, j):
        return pltpu.make_async_copy(
            sources[which].at[:, :, col(p, j)], place(which, j, my_rows), x_own.at[which, j]
        )

    def swap(which, j):
        return remote(
            sources[which].at[:, :, col(other, j)], place(which, j, my_rows),
            x_send.at[which, j], x_recv.at[which, j], to_other,
        )

    def halo_right(j):
        return remote(
            ext.at[j, :, pl.ds(F, W)], ext.at[j, :, pl.ds(0, W)], hr_send.at[j], hr_recv.at[j], to_right
        )

    def halo_left(j):
        return remote(
            ext.at[j, :, pl.ds(W, W)], ext.at[j, :, pl.ds(F + W, W)], hl_send.at[j], hl_recv.at[j], to_left
        )

    def key_copy(src, j, g, to):
        return remote(src, far.at[j, :, g], k_send.at[j, g], k_recv.at[j, g], to)

    def key_here(j, g, to):
        return key_copy(far.at[j, :, g], j, g, to)

    def sum_right_full(j):
        return remote(rsum.at[j], rsum.at[j], cr_send.at[j], cr_recv.at[j], to_right)

    def sum_right_first(j):
        part = rsum.at[j, pl.ds(0, F)]
        return remote(part, part, cr_send.at[j], cr_recv.at[j], to_right)

    def sum_right_last(j):
        return remote(edge_r.at[j], rsum.at[j, pl.ds(0, F)], cr_send.at[j], cr_recv.at[j], to_right)

    def sum_left_full(j):
        return remote(lsum.at[j], lsum.at[j], cl_send.at[j], cl_recv.at[j], to_left)

    def sum_left_first(j):
        part = lsum.at[j, pl.ds(0, F)]
        return remote(part, part, cl_send.at[j], cl_recv.at[j], to_left)

    def sum_left_last(j):
        return remote(edge_l.at[j], lsum.at[j, pl.ds(0, F)], cl_send.at[j], cl_recv.at[j], to_left)

    def query_left(j):
        return remote(
            rowbuf.at[j, pl.ds(0, F)], rowbuf.at[j, pl.ds(F, F)], q_send.at[j], q_recv.at[j], to_left
        )

    def out_own(j):
        return pltpu.make_async_copy(
            rowbuf.at[j, pl.ds(0, F), my_rows], out_ref.at[:, :, col(p, j)], o_own.at[j]
        )

    def out_other(j):
        return remote(
            rowbuf.at[j, pl.ds(0, F), other_rows], out_ref.at[:, :, col(p, j)], o_send.at[j], o_recv.at[j], to_other
        )

    barrier = pltpu.get_barrier_semaphore()
    pl.semaphore_signal(barrier, inc=1, device_id=to_other, device_id_type=MESH)

    @pl.when(has_right)
    def _():
        pl.semaphore_signal(barrier, inc=1, device_id=to_right, device_id_type=MESH)

    @pl.when(has_left)
    def _():
        pl.semaphore_signal(barrier, inc=1, device_id=to_left, device_id_type=MESH)

    pl.semaphore_wait(barrier, 1 + has_right.astype(jnp.int32) + has_left.astype(jnp.int32))

    def alone(half, j):
        if SHARED == 0:
            return j >= 0
        return jnp.where(half == 0, j < H - SHARED, j >= SHARED)

    def fetch(which, j):
        swap(which, j).start()
        own_copy(which, j).start()

    ahead = min(2, H)
    for first in range(ahead):
        fetch(1, first)
        fetch(2, first)

    def zero_halo(first):
        @pl.loop(0, H)
        def _(j):
            ext[j, :, first : first + W] = jnp.zeros((2, W, TOK, DH), jnp.float32)

    @pl.when(jnp.logical_not(has_left))
    def _():
        zero_halo(0)

    @pl.when(jnp.logical_not(has_right))
    def _():
        zero_halo(F + W)

    def arrive(which, j):
        own_copy(which, j).wait()
        swap(which, j).wait_recv()

    def compute(j):
        head = p * (H - SHARED) + j
        window = win_ref[head]
        stride = str_ref[head]
        for e in range(F + 2 * W):
            fill_split(ext[j, 0, e], ext[j, 1, e], ks, vs, e * TOK, TOK)

        def bias_row(flags):
            return jnp.concatenate(
                [jnp.full((1, TOK), jnp.where(ok, 0.0, NEG), jnp.float32) for ok in flags], axis=1
            )

        def wide_query(i):
            qh, ql = split_two(rowbuf[j, i] * (DH**-0.5))
            return jnp.concatenate([qh, ql, qh, ql], axis=1)

        @pl.when(jnp.logical_not(is_last))
        def _():
            far[j, :, z] = ext[j, :, W]
            far[j, :, z + 1] = ext[j, :, F + W]
            for g in range(Z):
                fill_split(far[j, 0, g], far[j, 1, g], kgs, vgs, g * TOK, TOK)
            far_bias = bias_row([((g * KSTRIDE) & (stride - 1)) == 0 for g in range(Z)])

            @pl.loop(0, jnp.where(is_helper, 2 * F, F))
            def _(i):
                dbuf[i] = soft_rows(wide_query(i), kgs[...], vgs[...], far_bias)

        @pl.when(is_last)
        def _():
            dbuf[0:F] = jnp.zeros((F, TOK, DH), jnp.float32)

        for i in range(F):
            flags = []
            for off in range(-W, W + 1):
                frame = z * F + i + off
                flags.append((abs(off) <= window) & (frame >= 0) & (frame < Z * F))
            near_rows = pl.ds(i * TOK, (2 * W + 1) * TOK)
            local = soft_rows(wide_query(i), ks[near_rows], vs[near_rows], bias_row(flags))
            rowbuf[j, i] = local
            dbuf[i] = dbuf[i] - local
        for c in range(NC):
            coef[j, c] = keep_of(j, c) * project([dbuf[i] for i in range(F)], z, c)

        @pl.when(is_helper)
        def _():
            for c in range(NC):
                more = project([dbuf[F + i] for i in range(F)], Z - 1, c)
                coef[j, c] = coef[j, c] + keep_of(j, c) * more

        @pl.when(is_first)
        def _():
            rsum[j, 0:F] = dbuf[0:F]

        @pl.when(is_last)
        def _():
            lsum[j, 0:F] = dbuf[0:F]

    def keep_of(j, c):
        return jnp.where((c + 1) // 2 <= cut_ref[p * (H - SHARED) + j], 1.0, 0.0)

    def project(frames, at, c):
        acc = frames[0] * basis_ref[at * F * NC + c]
        for i in range(1, F):
            acc = acc + frames[i] * basis_ref[(at * F + i) * NC + c]
        return acc

    def expand(start, totals, at, i):
        for c in range(NC):
            part = totals[c] * basis_ref[(at * F + i) * NC + c]
            start = part if start is None else start + part
        return start

    def finish(j):
        def ends(received):
            totals = [coef[j, c] for c in range(NC)]
            for i in range(F):
                rowbuf[j, i] = expand(rowbuf[j, i] + received[j, i], totals, z, i)

        @pl.when(is_first)
        def _():
            ends(lsum)

        @pl.when(is_last)
        def _():
            ends(rsum)

        @pl.when(has_left & has_right)
        def _():
            totals = [(rsum[j, c] - coef[j, c]) + lsum[j, c] for c in range(NC)]
            for i in range(F):
                rowbuf[j, i] = expand(rowbuf[j, i], totals, z, i)

        out_own(j).start()

        @pl.when(alone(p, j))
        def _():
            out_other(j).start()

    def add_raw(sums, j, at):
        raw = [sums[j, i] for i in range(F)]
        for c in range(NC):
            sums[j, c] = coef[j, c] + keep_of(j, c) * project(raw, at, c)

    def fill_edge(edge, sums, j, at):
        totals = [sums[j, c] for c in range(NC)]
        for i in range(F):
            edge[j, i] = expand(None, totals, at, i)

    from_first = z == 1
    middle_in_right = (z > 1) & (z < Z - 1)
    middle_in_left = (z > 0) & (z < Z - 2)
    middle_out_right = (z > 0) & (z < Z - 2)
    middle_out_left = (z > 1) & (z < Z - 1)

    def valid(j):
        return (j >= 0) & (j < H)

    @pl.loop(0, H)
    def _(t):
        arrive(1, t)
        arrive(2, t)

        @pl.when(t + ahead < H)
        def _():
            fetch(1, t + ahead)
            fetch(2, t + ahead)

        @pl.when(keys_right)
        def _():
            key_copy(ext.at[t, :, W], t, z, to_right).start()

        @pl.when(has_left)
        def _():
            halo_left(t).start()

        @pl.when(has_right)
        def _():
            halo_right(t).start()

    @pl.loop(0, H)
    def _(t):
        fetch(0, t)

    @pl.loop(0, H)
    def _(t):
        arrive(0, t)

        @pl.when(is_last)
        def _():
            query_left(t).start()

    @pl.loop(0, H + Z - 2)
    def _(t):
        @pl.when(valid(t) & has_right & has_left)
        def _():
            halo_left(t).wait_recv()
            key_copy(ext.at[t, :, F + W], t, z + 1, to_left).start()

        for d in range(1, Z - 1):
            @pl.when(valid(t - d + 1) & (z - d >= 0) & keys_right)
            def _():
                key_here(t - d + 1, z - d, to_right).wait_recv()
                key_here(t - d + 1, z - d, to_right).start()

        for d in range(2, Z):
            @pl.when(valid(t - d + 1) & (z + d < Z) & has_left)
            def _():
                key_here(t - d + 1, z + d, to_left).wait_recv()
                key_here(t - d + 1, z + d, to_left).start()

    reach = Z - 1
    right_delay = z
    left_delay = jnp.where(is_last, 0, 2 * reach - z)
    last_delay = jnp.maximum(right_delay, left_delay)

    @pl.loop(0, H + 2 * reach)
    def _(t):
        now = t

        @pl.when(valid(now))
        def _():
            @pl.when(has_left)
            def _():
                halo_right(now).wait_recv()

            @pl.when(is_first)
            def _():
                halo_left(now).wait_recv()
                for g in range(2, Z):
                    key_here(now, g, to_left).wait_recv()

            @pl.when(is_helper)
            def _():
                query_left(now).wait_recv()
                for g in range(Z - 2):
                    key_here(now, g, to_right).wait_recv()

            @pl.when(is_last)
            def _():
                query_left(now).wait_send()

            compute(now)

        jr = t - right_delay

        @pl.when(valid(jr))
        def _():
            @pl.when(is_first)
            def _():
                sum_right_first(jr).start()

            @pl.when(from_first)
            def _():
                sum_right_first(jr).wait_recv()
                add_raw(rsum, jr, 0)

            @pl.when(middle_in_right)
            def _():
                sum_right_full(jr).wait_recv()
                rsum[jr] = rsum[jr] + coef[jr]

            @pl.when(is_last)
            def _():
                sum_right_last(jr).wait_recv()

            @pl.when(middle_out_right)
            def _():
                sum_right_full(jr).start()

            @pl.when(is_helper)
            def _():
                fill_edge(edge_r, rsum, jr, Z - 1)
                sum_right_last(jr).start()

        jl = t - left_delay

        @pl.when(valid(jl))
        def _():
            @pl.when(is_last)
            def _():
                sum_left_first(jl).start()

            @pl.when(is_helper)
            def _():
                sum_left_first(jl).wait_recv()
                add_raw(lsum, jl, Z - 1)

            @pl.when(middle_in_left)
            def _():
                sum_left_full(jl).wait_recv()
                lsum[jl] = lsum[jl] + coef[jl]

            @pl.when(is_first)
            def _():
                sum_left_last(jl).wait_recv()

            @pl.when(middle_out_left)
            def _():
                sum_left_full(jl).start()

            @pl.when(from_first)
            def _():
                fill_edge(edge_l, lsum, jl, 0)
                sum_left_last(jl).start()

        jf = t - last_delay

        @pl.when(valid(jf))
        def _():
            finish(jf)

    @pl.loop(0, H)
    def _(j):
        for which in range(3):
            swap(which, j).wait_send()

        @pl.when(keys_right)
        def _():
            key_copy(ext.at[j, :, W], j, z, to_right).wait_send()

        @pl.when(has_right)
        def _():
            halo_right(j).wait_send()

        @pl.when(has_left)
        def _():
            halo_left(j).wait_send()

        @pl.when(is_first)
        def _():
            sum_right_first(j).wait_send()

        @pl.when(middle_out_right)
        def _():
            sum_right_full(j).wait_send()

        @pl.when(is_helper)
        def _():
            sum_right_last(j).wait_send()

        @pl.when(is_last)
        def _():
            sum_left_first(j).wait_send()

        @pl.when(middle_out_left)
        def _():
            sum_left_full(j).wait_send()

        @pl.when(from_first)
        def _():
            sum_left_last(j).wait_send()

        @pl.when(has_left & has_right)
        def _():
            key_copy(ext.at[j, :, F + W], j, z + 1, to_left).wait_send()

        for d in range(1, Z - 1):
            @pl.when((z - d >= 0) & keys_right)
            def _():
                key_here(j, z - d, to_right).wait_send()

        for d in range(2, Z):
            @pl.when((z + d < Z) & has_left)
            def _():
                key_here(j, z + d, to_left).wait_send()

        out_own(j).wait()

        @pl.when(alone(p, j))
        def _():
            out_other(j).wait_send()

        @pl.when(alone(other, j))
        def _():
            out_other(j).wait_recv()


def basis_table(total_frames, top):
    frames = np.arange(total_frames)
    columns = [np.full(total_frames, math.sqrt(1.0 / total_frames))]
    for k in range(1, top + 1):
        phase = 2.0 * math.pi * ((k * frames) % total_frames) / total_frames
        columns.append(math.sqrt(2.0 / total_frames) * np.cos(phase))
        columns.append(math.sqrt(2.0 / total_frames) * np.sin(phase))
    return np.stack(columns, axis=1).astype(np.float32)


def shards(queries, key_states, value_states, windows, strides, cutoffs):
    F, S, channels = queries.shape
    Z = lax.axis_size("frm")
    heads = channels // DH
    H = (heads + 1) // 2
    SHARED = 2 * H - heads
    W = F // 2
    basis = basis_table(F * Z, F * Z // 8)
    NC = basis.shape[1]
    assert lax.axis_size("pos") == 2 and F == KSTRIDE and Z >= 3 and NC >= F
    TOK = 2 * S
    dma = pltpu.SemaphoreType.DMA
    f32, bf16 = jnp.float32, jnp.bfloat16
    return pl.pallas_call(
        functools.partial(kernel, (F, S, H, SHARED, Z, W, NC)),
        out_shape=jax.ShapeDtypeStruct(queries.shape, f32),
        in_specs=[pl.BlockSpec(memory_space=pltpu.SMEM)] * 4 + [pl.BlockSpec(memory_space=pl.ANY)] * 3,
        out_specs=pl.BlockSpec(memory_space=pl.ANY),
        scratch_shapes=[
            pltpu.VMEM((H, 2, F + 2 * W, TOK, DH), f32),
            pltpu.VMEM((H, 2, Z, TOK, DH), f32),
            pltpu.VMEM((H, 2 * F, TOK, DH), f32),
            pltpu.VMEM((H, NC, TOK, DH), f32),
            pltpu.VMEM((H, NC, TOK, DH), f32),
            pltpu.VMEM((H, NC, TOK, DH), f32),
            pltpu.VMEM((H, F, TOK, DH), f32),
            pltpu.VMEM((H, F, TOK, DH), f32),
            pltpu.VMEM((2 * F, TOK, DH), f32),
            pltpu.VMEM(((F + 2 * W) * TOK, 4 * DH), bf16),
            pltpu.VMEM(((F + 2 * W) * TOK, 2 * DH), bf16),
            pltpu.VMEM((Z * TOK, 4 * DH), bf16),
            pltpu.VMEM((Z * TOK, 2 * DH), bf16),
            dma((3, H)), dma((3, H)), dma((3, H)),
            dma((H,)), dma((H,)), dma((H,)), dma((H,)),
            dma((H, Z)), dma((H, Z)),
            dma((H,)), dma((H,)), dma((H,)), dma((H,)),
            dma((H,)), dma((H,)), dma((H,)), dma((H,)), dma((H,)),
        ],
        compiler_params=pltpu.CompilerParams(
            collective_id=0, has_side_effects=True, vmem_limit_bytes=60 * 1024 * 1024
        ),
    )(windows, strides, cutoffs, jnp.asarray(basis.reshape(-1)), queries, key_states, value_states)


def solution(mesh):
    in_specs = (
        P(("grp", "frm"), "pos", "head"),
        P(("grp", "frm"), "pos", "head"),
        P(("grp", "frm"), "pos", "head"),
        P("head"),
        P("head"),
        P("head"),
    )
    out_specs = P(("grp", "frm"), "pos", "head")
    return jax.shard_map(shards, mesh=mesh, in_specs=in_specs, out_specs=out_specs, check_vma=False)
```

```python
import functools
import math

import jax
import jax.numpy as jnp
import numpy as np
from jax import lax
from jax.experimental import pallas as pl
from jax.experimental.pallas import tpu as pltpu
from jax.sharding import PartitionSpec as P

DH = 128
KSTRIDE = 4
MESH = pl.DeviceIdType.MESH
NEG = -1e30


def split_two(x):
    high = x.astype(jnp.bfloat16)
    low = (x - high.astype(jnp.float32)).astype(jnp.bfloat16)
    return high, low


def soft_rows(q_wide, keys, values, bias):
    rows = q_wide.shape[0]
    scores = lax.dot_general(
        q_wide, keys, (((1,), (1,)), ((), ())), preferred_element_type=jnp.float32
    )
    scores = scores + bias
    highest = jnp.max(scores, axis=1, keepdims=True)
    weights = jnp.exp(scores - highest)
    total = jnp.sum(weights, axis=1, keepdims=True)
    both = jnp.concatenate(split_two(weights), axis=0)
    wide = jnp.dot(both, values, preferred_element_type=jnp.float32)
    summed = (wide[:rows, :DH] + wide[:rows, DH:]) + (wide[rows:, :DH] + wide[rows:, DH:])
    return summed / total


def fill_split(key, value, keys_wide, values_wide, row, count):
    kh, kl = split_two(key)
    vh, vl = split_two(value)
    rows = pl.ds(row, count)
    keys_wide[rows, 0:DH] = kh
    keys_wide[rows, DH : 2 * DH] = kh
    keys_wide[rows, 2 * DH : 3 * DH] = kl
    keys_wide[rows, 3 * DH : 4 * DH] = kl
    values_wide[rows, 0:DH] = vh
    values_wide[rows, DH : 2 * DH] = vl


def kernel(
    sizes,
    win_ref, str_ref, cut_ref, basis_ref, q_ref, k_ref, v_ref, out_ref,
    ext, far, rowbuf, coef, rsum, lsum, edge_r, edge_l, dbuf, ks, vs, kgs, vgs,
    x_own, x_send, x_recv, hr_send, hr_recv, hl_send, hl_recv, k_send, k_recv,
    cr_send, cr_recv, cl_send, cl_recv, q_send, q_recv, o_own, o_send, o_recv,
):
    F, S, H, SHARED, Z, W, NC = sizes
    TOK = 2 * S
    z = lax.axis_index("frm")
    p = lax.axis_index("pos")
    other = 1 - p
    has_right = z < Z - 1
    has_left = z > 0
    right = jnp.minimum(z + 1, Z - 1)
    left = jnp.maximum(z - 1, 0)
    is_first = z == 0
    is_last = z == Z - 1
    is_helper = z == Z - 2
    keys_right = z < Z - 2
    to_right, to_left, to_other = {"frm": right}, {"frm": left}, {"pos": other}

    def remote(src, dst, send, recv, to):
        return pltpu.make_async_remote_copy(
            src_ref=src, dst_ref=dst, send_sem=send, recv_sem=recv, device_id=to, device_id_type=MESH
        )

    def col(half, j):
        return pl.ds(pl.multiple_of((half * (H - SHARED) + j) * DH, DH), DH)

    my_rows = pl.ds(pl.multiple_of(p * S, S), S)
    other_rows = pl.ds(pl.multiple_of(other * S, S), S)

    def place(which, j, rows):
        if which == 0:
            return rowbuf.at[j, pl.ds(0, F), rows]
        return ext.at[j, which - 1, pl.ds(W, F), rows]

    sources = (q_ref, k_ref, v_ref)

    def own_copy(which, j):
        return pltpu.make_async_copy(
            sources[which].at[:, :, col(p, j)], place(which, j, my_rows), x_own.at[which, j]
        )

    def swap(which, j):
        return remote(
            sources[which].at[:, :, col(other, j)], place(which, j, my_rows),
            x_send.at[which, j], x_recv.at[which, j], to_other,
        )

    def halo_right(j):
        return remote(
            ext.at[j, :, pl.ds(F, W)], ext.at[j, :, pl.ds(0, W)], hr_send.at[j], hr_recv.at[j], to_right
        )

    def halo_left(j):
        return remote(
            ext.at[j, :, pl.ds(W, W)], ext.at[j, :, pl.ds(F + W, W)], hl_send.at[j], hl_recv.at[j], to_left
        )

    def key_copy(src, j, g, to):
        return remote(src, far.at[j, :, g], k_send.at[j, g], k_recv.at[j, g], to)

    def key_here(j, g, to):
        return key_copy(far.at[j, :, g], j, g, to)

    def sum_right_full(j):
        return remote(rsum.at[j], rsum.at[j], cr_send.at[j], cr_recv.at[j], to_right)

    def sum_right_first(j):
        part = rsum.at[j, pl.ds(0, F)]
        return remote(part, part, cr_send.at[j], cr_recv.at[j], to_right)

    def sum_right_last(j):
        return remote(edge_r.at[j], rsum.at[j, pl.ds(0, F)], cr_send.at[j], cr_recv.at[j], to_right)

    def sum_left_full(j):
        return remote(lsum.at[j], lsum.at[j], cl_send.at[j], cl_recv.at[j], to_left)

    def sum_left_first(j):
        part = lsum.at[j, pl.ds(0, F)]
        return remote(part, part, cl_send.at[j], cl_recv.at[j], to_left)

    def sum_left_last(j):
        return remote(edge_l.at[j], lsum.at[j, pl.ds(0, F)], cl_send.at[j], cl_recv.at[j], to_left)

    def query_left(j):
        return remote(
            rowbuf.at[j, pl.ds(0, F)], rowbuf.at[j, pl.ds(F, F)], q_send.at[j], q_recv.at[j], to_left
        )

    def out_own(j):
        return pltpu.make_async_copy(
            rowbuf.at[j, pl.ds(0, F), my_rows], out_ref.at[:, :, col(p, j)], o_own.at[j]
        )

    def out_other(j):
        return remote(
            rowbuf.at[j, pl.ds(0, F), other_rows], out_ref.at[:, :, col(p, j)], o_send.at[j], o_recv.at[j], to_other
        )

    barrier = pltpu.get_barrier_semaphore()
    pl.semaphore_signal(barrier, inc=1, device_id=to_other, device_id_type=MESH)

    @pl.when(has_right)
    def _():
        pl.semaphore_signal(barrier, inc=1, device_id=to_right, device_id_type=MESH)

    @pl.when(has_left)
    def _():
        pl.semaphore_signal(barrier, inc=1, device_id=to_left, device_id_type=MESH)

    pl.semaphore_wait(barrier, 1 + has_right.astype(jnp.int32) + has_left.astype(jnp.int32))

    def alone(half, j):
        if SHARED == 0:
            return j >= 0
        return jnp.where(half == 0, j < H - SHARED, j >= SHARED)

    def fetch(which, j):
        swap(which, j).start()
        own_copy(which, j).start()

    ahead = min(2, H)
    for first in range(ahead):
        for which in (1, 2, 0):
            fetch(which, first)

    def zero_halo(first):
        @pl.loop(0, H)
        def _(j):
            ext[j, :, first : first + W] = jnp.zeros((2, W, TOK, DH), jnp.float32)

    @pl.when(jnp.logical_not(has_left))
    def _():
        zero_halo(0)

    @pl.when(jnp.logical_not(has_right))
    def _():
        zero_halo(F + W)

    def arrive(which, j):
        own_copy(which, j).wait()
        swap(which, j).wait_recv()

    def compute(j):
        head = p * (H - SHARED) + j
        window = win_ref[head]
        stride = str_ref[head]
        for e in range(F + 2 * W):
            fill_split(ext[j, 0, e], ext[j, 1, e], ks, vs, e * TOK, TOK)

        def bias_row(flags):
            return jnp.concatenate(
                [jnp.full((1, TOK), jnp.where(ok, 0.0, NEG), jnp.float32) for ok in flags], axis=1
            )

        def wide_query(i):
            qh, ql = split_two(rowbuf[j, i] * (DH**-0.5))
            return jnp.concatenate([qh, ql, qh, ql], axis=1)

        @pl.when(jnp.logical_not(is_last))
        def _():
            far[j, :, z] = ext[j, :, W]
            far[j, :, z + 1] = ext[j, :, F + W]
            for g in range(Z):
                fill_split(far[j, 0, g], far[j, 1, g], kgs, vgs, g * TOK, TOK)
            far_bias = bias_row([((g * KSTRIDE) & (stride - 1)) == 0 for g in range(Z)])

            @pl.loop(0, jnp.where(is_helper, 2 * F, F))
            def _(i):
                dbuf[i] = soft_rows(wide_query(i), kgs[...], vgs[...], far_bias)

        @pl.when(is_last)
        def _():
            dbuf[0:F] = jnp.zeros((F, TOK, DH), jnp.float32)

        for i in range(F):
            flags = []
            for off in range(-W, W + 1):
                frame = z * F + i + off
                flags.append((abs(off) <= window) & (frame >= 0) & (frame < Z * F))
            near_rows = pl.ds(i * TOK, (2 * W + 1) * TOK)
            local = soft_rows(wide_query(i), ks[near_rows], vs[near_rows], bias_row(flags))
            rowbuf[j, i] = local
            dbuf[i] = dbuf[i] - local
        for c in range(NC):
            coef[j, c] = keep_of(j, c) * project([dbuf[i] for i in range(F)], z, c)

        @pl.when(is_helper)
        def _():
            for c in range(NC):
                more = project([dbuf[F + i] for i in range(F)], Z - 1, c)
                coef[j, c] = coef[j, c] + keep_of(j, c) * more

        @pl.when(is_first)
        def _():
            rsum[j, 0:F] = dbuf[0:F]

        @pl.when(is_last)
        def _():
            lsum[j, 0:F] = dbuf[0:F]

    def keep_of(j, c):
        return jnp.where((c + 1) // 2 <= cut_ref[p * (H - SHARED) + j], 1.0, 0.0)

    def project(frames, at, c):
        acc = frames[0] * basis_ref[at * F * NC + c]
        for i in range(1, F):
            acc = acc + frames[i] * basis_ref[(at * F + i) * NC + c]
        return acc

    def expand(start, totals, at, i):
        for c in range(NC):
            part = totals[c] * basis_ref[(at * F + i) * NC + c]
            start = part if start is None else start + part
        return start

    def finish(j):
        def ends(received):
            totals = [coef[j, c] for c in range(NC)]
            for i in range(F):
                rowbuf[j, i] = expand(rowbuf[j, i] + received[j, i], totals, z, i)

        @pl.when(is_first)
        def _():
            ends(lsum)

        @pl.when(is_last)
        def _():
            ends(rsum)

        @pl.when(has_left & has_right)
        def _():
            totals = [(rsum[j, c] - coef[j, c]) + lsum[j, c] for c in range(NC)]
            for i in range(F):
                rowbuf[j, i] = expand(rowbuf[j, i], totals, z, i)

        out_own(j).start()

        @pl.when(alone(p, j))
        def _():
            out_other(j).start()

    def add_raw(sums, j, at):
        raw = [sums[j, i] for i in range(F)]
        for c in range(NC):
            sums[j, c] = coef[j, c] + keep_of(j, c) * project(raw, at, c)

    def fill_edge(edge, sums, j, at):
        totals = [sums[j, c] for c in range(NC)]
        for i in range(F):
            edge[j, i] = expand(None, totals, at, i)

    delay = jnp.where(is_last, 1, jnp.where(is_first | is_helper, Z - 2, jnp.maximum(z, Z - 1 - z)))
    right_delay = jnp.where(is_last, 2 * Z - 2, Z - 2 + z)
    left_delay = jnp.where(is_last, 2, Z - 1 + 2 * (Z - 2 - z))
    last_delay = jnp.maximum(right_delay, left_delay)
    from_first = z == 1
    middle_in_right = (z > 1) & (z < Z - 1)
    middle_in_left = (z > 0) & (z < Z - 2)
    middle_out_right = (z > 0) & (z < Z - 2)
    middle_out_left = (z > 1) & (z < Z - 1)

    def valid(j):
        return (j >= 0) & (j < H)

    @pl.loop(0, H + 3 * Z - 5)
    def _(t):
        @pl.when(t < H)
        def _():
            arrive(1, t)
            arrive(2, t)

            @pl.when(t + ahead < H)
            def _():
                for which in (1, 2, 0):
                    fetch(which, t + ahead)

            @pl.when(keys_right)
            def _():
                key_copy(ext.at[t, :, W], t, z, to_right).start()

            @pl.when(has_right)
            def _():
                halo_right(t).start()

            @pl.when(has_left)
            def _():
                halo_left(t).start()

            arrive(0, t)

        @pl.when(valid(t - 1) & is_last)
        def _():
            query_left(t - 1).start()

        @pl.when(valid(t - 1) & has_right & has_left)
        def _():
            halo_left(t - 1).wait_recv()
            key_copy(ext.at[t - 1, :, F + W], t - 1, z + 1, to_left).start()

        for d in range(1, Z - 1):
            @pl.when(valid(t - d) & (z - d >= 0) & keys_right)
            def _():
                key_here(t - d, z - d, to_right).wait_recv()
                key_here(t - d, z - d, to_right).start()

        for d in range(2, Z):
            @pl.when(valid(t - d) & (z + d < Z) & has_left)
            def _():
                key_here(t - d, z + d, to_left).wait_recv()
                key_here(t - d, z + d, to_left).start()

        now = t - delay

        @pl.when(valid(now))
        def _():
            @pl.when(has_left)
            def _():
                halo_right(now).wait_recv()

            @pl.when(is_first)
            def _():
                halo_left(now).wait_recv()
                for g in range(2, Z):
                    key_here(now, g, to_left).wait_recv()

            @pl.when(is_helper)
            def _():
                query_left(now).wait_recv()
                for g in range(Z - 2):
                    key_here(now, g, to_right).wait_recv()

            @pl.when(is_last)
            def _():
                query_left(now).wait_send()

            compute(now)

        jl = t - left_delay

        @pl.when(valid(jl))
        def _():
            @pl.when(is_last)
            def _():
                sum_left_first(jl).start()

            @pl.when(is_helper)
            def _():
                sum_left_first(jl).wait_recv()
                add_raw(lsum, jl, Z - 1)

            @pl.when(middle_in_left)
            def _():
                sum_left_full(jl).wait_recv()
                lsum[jl] = lsum[jl] + coef[jl]

            @pl.when(is_first)
            def _():
                sum_left_last(jl).wait_recv()

            @pl.when(middle_out_left)
            def _():
                sum_left_full(jl).start()

            @pl.when(from_first)
            def _():
                fill_edge(edge_l, lsum, jl, 0)
                sum_left_last(jl).start()

        jr = t - right_delay

        @pl.when(valid(jr))
        def _():
            @pl.when(is_first)
            def _():
                sum_right_first(jr).start()

            @pl.when(from_first)
            def _():
                sum_right_first(jr).wait_recv()
                add_raw(rsum, jr, 0)

            @pl.when(middle_in_right)
            def _():
                sum_right_full(jr).wait_recv()
                rsum[jr] = rsum[jr] + coef[jr]

            @pl.when(is_last)
            def _():
                sum_right_last(jr).wait_recv()

            @pl.when(middle_out_right)
            def _():
                sum_right_full(jr).start()

            @pl.when(is_helper)
            def _():
                fill_edge(edge_r, rsum, jr, Z - 1)
                sum_right_last(jr).start()

        jf = t - last_delay

        @pl.when(valid(jf))
        def _():
            finish(jf)

    @pl.loop(0, H)
    def _(j):
        for which in range(3):
            swap(which, j).wait_send()

        @pl.when(keys_right)
        def _():
            key_copy(ext.at[j, :, W], j, z, to_right).wait_send()

        @pl.when(has_right)
        def _():
            halo_right(j).wait_send()

        @pl.when(has_left)
        def _():
            halo_left(j).wait_send()

        @pl.when(is_first)
        def _():
            sum_right_first(j).wait_send()

        @pl.when(middle_out_right)
        def _():
            sum_right_full(j).wait_send()

        @pl.when(is_helper)
        def _():
            sum_right_last(j).wait_send()

        @pl.when(is_last)
        def _():
            sum_left_first(j).wait_send()

        @pl.when(middle_out_left)
        def _():
            sum_left_full(j).wait_send()

        @pl.when(from_first)
        def _():
            sum_left_last(j).wait_send()

        @pl.when(has_left & has_right)
        def _():
            key_copy(ext.at[j, :, F + W], j, z + 1, to_left).wait_send()

        for d in range(1, Z - 1):
            @pl.when((z - d >= 0) & keys_right)
            def _():
                key_here(j, z - d, to_right).wait_send()

        for d in range(2, Z):
            @pl.when((z + d < Z) & has_left)
            def _():
                key_here(j, z + d, to_left).wait_send()

        out_own(j).wait()

        @pl.when(alone(p, j))
        def _():
            out_other(j).wait_send()

        @pl.when(alone(other, j))
        def _():
            out_other(j).wait_recv()


def basis_table(total_frames, top):
    frames = np.arange(total_frames)
    columns = [np.full(total_frames, math.sqrt(1.0 / total_frames))]
    for k in range(1, top + 1):
        phase = 2.0 * math.pi * ((k * frames) % total_frames) / total_frames
        columns.append(math.sqrt(2.0 / total_frames) * np.cos(phase))
        columns.append(math.sqrt(2.0 / total_frames) * np.sin(phase))
    return np.stack(columns, axis=1).astype(np.float32)


def shards(queries, key_states, value_states, windows, strides, cutoffs):
    F, S, channels = queries.shape
    Z = lax.axis_size("frm")
    heads = channels // DH
    H = (heads + 1) // 2
    SHARED = 2 * H - heads
    W = F // 2
    basis = basis_table(F * Z, F * Z // 8)
    NC = basis.shape[1]
    assert lax.axis_size("pos") == 2 and F == KSTRIDE and Z >= 3 and NC >= F
    TOK = 2 * S
    dma = pltpu.SemaphoreType.DMA
    f32, bf16 = jnp.float32, jnp.bfloat16
    return pl.pallas_call(
        functools.partial(kernel, (F, S, H, SHARED, Z, W, NC)),
        out_shape=jax.ShapeDtypeStruct(queries.shape, f32),
        in_specs=[pl.BlockSpec(memory_space=pltpu.SMEM)] * 4 + [pl.BlockSpec(memory_space=pl.ANY)] * 3,
        out_specs=pl.BlockSpec(memory_space=pl.ANY),
        scratch_shapes=[
            pltpu.VMEM((H, 2, F + 2 * W, TOK, DH), f32),
            pltpu.VMEM((H, 2, Z, TOK, DH), f32),
            pltpu.VMEM((H, 2 * F, TOK, DH), f32),
            pltpu.VMEM((H, NC, TOK, DH), f32),
            pltpu.VMEM((H, NC, TOK, DH), f32),
            pltpu.VMEM((H, NC, TOK, DH), f32),
            pltpu.VMEM((H, F, TOK, DH), f32),
            pltpu.VMEM((H, F, TOK, DH), f32),
            pltpu.VMEM((2 * F, TOK, DH), f32),
            pltpu.VMEM(((F + 2 * W) * TOK, 4 * DH), bf16),
            pltpu.VMEM(((F + 2 * W) * TOK, 2 * DH), bf16),
            pltpu.VMEM((Z * TOK, 4 * DH), bf16),
            pltpu.VMEM((Z * TOK, 2 * DH), bf16),
            dma((3, H)), dma((3, H)), dma((3, H)),
            dma((H,)), dma((H,)), dma((H,)), dma((H,)),
            dma((H, Z)), dma((H, Z)),
            dma((H,)), dma((H,)), dma((H,)), dma((H,)),
            dma((H,)), dma((H,)), dma((H,)), dma((H,)), dma((H,)),
        ],
        compiler_params=pltpu.CompilerParams(
            collective_id=0, has_side_effects=True, vmem_limit_bytes=60 * 1024 * 1024
        ),
    )(windows, strides, cutoffs, jnp.asarray(basis.reshape(-1)), queries, key_states, value_states)


def solution(mesh):
    in_specs = (
        P(("grp", "frm"), "pos", "head"),
        P(("grp", "frm"), "pos", "head"),
        P(("grp", "frm"), "pos", "head"),
        P("head"),
        P("head"),
        P("head"),
    )
    out_specs = P(("grp", "frm"), "pos", "head")
    return jax.shard_map(shards, mesh=mesh, in_specs=in_specs, out_specs=out_specs, check_vma=False)
```

```python
import functools
import math

import jax
import jax.numpy as jnp
import numpy as np
from jax import lax
from jax.experimental import pallas as pl
from jax.experimental.pallas import tpu as pltpu
from jax.sharding import PartitionSpec as P

DH = 128
KSTRIDE = 4
MESH = pl.DeviceIdType.MESH
NEG = -1e30


def split_two(x):
    high = x.astype(jnp.bfloat16)
    low = (x - high.astype(jnp.float32)).astype(jnp.bfloat16)
    return high, low


def score_rows(q_wide, keys):
    return jnp.dot(q_wide, keys, preferred_element_type=jnp.float32)


def soft(scores, bias):
    scores = scores + bias
    weights = jnp.exp2(scores - jnp.max(scores, axis=1, keepdims=True))
    return weights, jnp.sum(weights, axis=1, keepdims=True)


def weigh(weights, total, values):
    rows = weights.shape[0]
    both = jnp.concatenate(split_two(weights), axis=0)
    wide = jnp.dot(both, values, preferred_element_type=jnp.float32)
    summed = (wide[:rows, :DH] + wide[:rows, DH:]) + (wide[rows:, :DH] + wide[rows:, DH:])
    return summed / total


def fill_split(key, value, keys_wide, values_wide, row, count):
    kh, kl = split_two(key.T)
    vh, vl = split_two(value)
    rows = pl.ds(row, count)
    keys_wide[0:DH, rows] = kh
    keys_wide[DH : 2 * DH, rows] = kh
    keys_wide[2 * DH : 3 * DH, rows] = kl
    keys_wide[3 * DH : 4 * DH, rows] = kl
    values_wide[rows, 0:DH] = vh
    values_wide[rows, DH : 2 * DH] = vl


def kernel(
    sizes,
    win_ref, str_ref, cut_ref, basis_ref, q_ref, k_ref, v_ref, out_ref,
    ext, far, rowbuf, coef, rsum, lsum, edge_r, edge_l, dbuf, ks, vs, kgs, vgs,
    x_own, x_send, x_recv, hr_send, hr_recv, hl_send, hl_recv, k_send, k_recv,
    cr_send, cr_recv, cl_send, cl_recv, q_send, q_recv, o_own, o_send, o_recv,
):
    F, S, H, SHARED, Z, W, NC = sizes
    TOK = 2 * S
    z = lax.axis_index("frm")
    p = lax.axis_index("pos")
    other = 1 - p
    has_right = z < Z - 1
    has_left = z > 0
    right = jnp.minimum(z + 1, Z - 1)
    left = jnp.maximum(z - 1, 0)
    is_first = z == 0
    is_last = z == Z - 1
    is_helper = z == Z - 2
    keys_right = z < Z - 2
    to_right, to_left, to_other = {"frm": right}, {"frm": left}, {"pos": other}

    def remote(src, dst, send, recv, to):
        return pltpu.make_async_remote_copy(
            src_ref=src, dst_ref=dst, send_sem=send, recv_sem=recv, device_id=to, device_id_type=MESH
        )

    def col(half, j):
        return pl.ds(pl.multiple_of((half * (H - SHARED) + j) * DH, DH), DH)

    my_rows = pl.ds(pl.multiple_of(p * S, S), S)
    other_rows = pl.ds(pl.multiple_of(other * S, S), S)

    def place(which, j, rows):
        if which == 0:
            return rowbuf.at[j, pl.ds(0, F), rows]
        return ext.at[j, which - 1, pl.ds(W, F), rows]

    sources = (q_ref, k_ref, v_ref)

    def own_copy(which, j):
        return pltpu.make_async_copy(
            sources[which].at[:, :, col(p, j)], place(which, j, my_rows), x_own.at[which, j]
        )

    def swap(which, j):
        return remote(
            sources[which].at[:, :, col(other, j)], place(which, j, my_rows),
            x_send.at[which, j], x_recv.at[which, j], to_other,
        )

    def halo_right(j):
        return remote(
            ext.at[j, :, pl.ds(F, W)], ext.at[j, :, pl.ds(0, W)], hr_send.at[j], hr_recv.at[j], to_right
        )

    def halo_left(j):
        return remote(
            ext.at[j, :, pl.ds(W, W)], ext.at[j, :, pl.ds(F + W, W)], hl_send.at[j], hl_recv.at[j], to_left
        )

    def key_copy(src, j, g, to):
        return remote(src, far.at[j, :, g], k_send.at[j, g], k_recv.at[j, g], to)

    def key_here(j, g, to):
        return key_copy(far.at[j, :, g], j, g, to)

    def sum_right_full(j):
        return remote(rsum.at[j], rsum.at[j], cr_send.at[j], cr_recv.at[j], to_right)

    def sum_right_first(j):
        part = rsum.at[j, pl.ds(0, F)]
        return remote(part, part, cr_send.at[j], cr_recv.at[j], to_right)

    def sum_right_last(j):
        return remote(edge_r.at[j], rsum.at[j, pl.ds(0, F)], cr_send.at[j], cr_recv.at[j], to_right)

    def sum_left_full(j):
        return remote(lsum.at[j], lsum.at[j], cl_send.at[j], cl_recv.at[j], to_left)

    def sum_left_first(j):
        part = lsum.at[j, pl.ds(0, F)]
        return remote(part, part, cl_send.at[j], cl_recv.at[j], to_left)

    def sum_left_last(j):
        return remote(edge_l.at[j], lsum.at[j, pl.ds(0, F)], cl_send.at[j], cl_recv.at[j], to_left)

    def query_left(j):
        return remote(
            rowbuf.at[j, pl.ds(0, F)], rowbuf.at[j, pl.ds(F, F)], q_send.at[j], q_recv.at[j], to_left
        )

    def out_own(j):
        return pltpu.make_async_copy(
            rowbuf.at[j, pl.ds(0, F), my_rows], out_ref.at[:, :, col(p, j)], o_own.at[j]
        )

    def out_other(j):
        return remote(
            rowbuf.at[j, pl.ds(0, F), other_rows], out_ref.at[:, :, col(p, j)], o_send.at[j], o_recv.at[j], to_other
        )

    barrier = pltpu.get_barrier_semaphore()
    pl.semaphore_signal(barrier, inc=1, device_id=to_other, device_id_type=MESH)

    @pl.when(has_right)
    def _():
        pl.semaphore_signal(barrier, inc=1, device_id=to_right, device_id_type=MESH)

    @pl.when(has_left)
    def _():
        pl.semaphore_signal(barrier, inc=1, device_id=to_left, device_id_type=MESH)

    pl.semaphore_wait(barrier, 1 + has_right.astype(jnp.int32) + has_left.astype(jnp.int32))

    def alone(half, j):
        if SHARED == 0:
            return j >= 0
        return jnp.where(half == 0, j < H - SHARED, j >= SHARED)

    def fetch(which, j):
        swap(which, j).start()
        own_copy(which, j).start()

    ahead = min(2, H)
    for first in range(ahead):
        for which in (1, 2, 0):
            fetch(which, first)

    def zero_halo(first):
        @pl.loop(0, H)
        def _(j):
            ext[j, :, first : first + W] = jnp.zeros((2, W, TOK, DH), jnp.float32)

    @pl.when(jnp.logical_not(has_left))
    def _():
        zero_halo(0)

    @pl.when(jnp.logical_not(has_right))
    def _():
        zero_halo(F + W)

    def arrive(which, j):
        own_copy(which, j).wait()
        swap(which, j).wait_recv()

    def compute(j):
        head = p * (H - SHARED) + j
        window = win_ref[head]
        stride = str_ref[head]
        for e in range(F + 2 * W):
            fill_split(ext[j, 0, e], ext[j, 1, e], ks, vs, e * TOK, TOK)

        def bias_row(flags):
            return jnp.concatenate(
                [jnp.full((1, TOK), jnp.where(ok, 0.0, NEG), jnp.float32) for ok in flags], axis=1
            )

        def wide_query(i):
            both = rowbuf[j, pl.ds(i, 2)].reshape(2 * TOK, DH)
            qh, ql = split_two(both * (DH**-0.5 * math.log2(math.e)))
            return jnp.concatenate([qh, ql, qh, ql], axis=1)

        def near_pair(i, q_wide):
            span = (2 * W + 1) * TOK
            rows = pl.ds(i * TOK, span + TOK)
            scores = score_rows(q_wide, ks[:, rows])
            parts, totals = [], []
            for u in range(2):
                flags = []
                for off in range(-W, W + 1):
                    frame = z * F + i + u + off
                    flags.append((abs(off) <= window) & (frame >= 0) & (frame < Z * F))
                part = scores[u * TOK : (u + 1) * TOK, u * TOK : u * TOK + span]
                weights, total = soft(part, bias_row(flags))
                empty = jnp.zeros((TOK, TOK), jnp.float32)
                pieces = [weights, empty] if u == 0 else [empty, weights]
                parts.append(jnp.concatenate(pieces, axis=1))
                totals.append(total)
            return weigh(jnp.concatenate(parts, axis=0), jnp.concatenate(totals, axis=0), vs[rows])

        def far_pair(q_wide, far_bias):
            weights, total = soft(score_rows(q_wide, kgs[...]), far_bias)
            return weigh(weights, total, vgs[...])

        def keep_pair(i, local, wide):
            local = local.reshape(2, TOK, DH)
            rowbuf[j, i : i + 2] = local
            dbuf[i : i + 2] = -local if wide is None else wide.reshape(2, TOK, DH) - local

        @pl.when(jnp.logical_not(is_last))
        def _():
            far[j, :, z] = ext[j, :, W]
            far[j, :, z + 1] = ext[j, :, F + W]
            for g in range(Z):
                fill_split(far[j, 0, g], far[j, 1, g], kgs, vgs, g * TOK, TOK)
            far_bias = bias_row([((g * KSTRIDE) & (stride - 1)) == 0 for g in range(Z)])
            for i in range(0, F, 2):
                q_wide = wide_query(i)
                keep_pair(i, near_pair(i, q_wide), far_pair(q_wide, far_bias))

            @pl.when(is_helper)
            def _():
                for i in range(F, 2 * F, 2):
                    wide = far_pair(wide_query(i), far_bias)
                    dbuf[i : i + 2] = wide.reshape(2, TOK, DH)

        @pl.when(is_last)
        def _():
            for i in range(0, F, 2):
                keep_pair(i, near_pair(i, wide_query(i)), None)

        for c in range(NC):
            coef[j, c] = keep_of(j, c) * project([dbuf[i] for i in range(F)], z, c)

        @pl.when(is_helper)
        def _():
            for c in range(NC):
                more = project([dbuf[F + i] for i in range(F)], Z - 1, c)
                coef[j, c] = coef[j, c] + keep_of(j, c) * more

        @pl.when(is_first)
        def _():
            rsum[j, 0:F] = dbuf[0:F]

        @pl.when(is_last)
        def _():
            lsum[j, 0:F] = dbuf[0:F]

    def keep_of(j, c):
        return jnp.where((c + 1) // 2 <= cut_ref[p * (H - SHARED) + j], 1.0, 0.0)

    def project(frames, at, c):
        acc = frames[0] * basis_ref[at * F * NC + c]
        for i in range(1, F):
            acc = acc + frames[i] * basis_ref[(at * F + i) * NC + c]
        return acc

    def expand(start, totals, at, i):
        for c in range(NC):
            part = totals[c] * basis_ref[(at * F + i) * NC + c]
            start = part if start is None else start + part
        return start

    def finish(j):
        def ends(received):
            totals = [coef[j, c] for c in range(NC)]
            for i in range(F):
                rowbuf[j, i] = expand(rowbuf[j, i] + received[j, i], totals, z, i)

        @pl.when(is_first)
        def _():
            ends(lsum)

        @pl.when(is_last)
        def _():
            ends(rsum)

        @pl.when(has_left & has_right)
        def _():
            totals = [(rsum[j, c] - coef[j, c]) + lsum[j, c] for c in range(NC)]
            for i in range(F):
                rowbuf[j, i] = expand(rowbuf[j, i], totals, z, i)

        out_own(j).start()

        @pl.when(alone(p, j))
        def _():
            out_other(j).start()

    def add_raw(sums, j, at):
        raw = [sums[j, i] for i in range(F)]
        for c in range(NC):
            sums[j, c] = coef[j, c] + keep_of(j, c) * project(raw, at, c)

    def fill_edge(edge, sums, j, at):
        totals = [sums[j, c] for c in range(NC)]
        for i in range(F):
            edge[j, i] = expand(None, totals, at, i)

    delay = jnp.where(is_last, 1, jnp.where(is_first | is_helper, Z - 2, jnp.maximum(z, Z - 1 - z)))
    right_delay = jnp.where(is_last, 2 * Z - 2, Z - 2 + z)
    left_delay = jnp.where(is_last, 2, Z - 1 + 2 * (Z - 2 - z))
    last_delay = jnp.maximum(right_delay, left_delay)
    from_first = z == 1
    middle_in_right = (z > 1) & (z < Z - 1)
    middle_in_left = (z > 0) & (z < Z - 2)
    middle_out_right = (z > 0) & (z < Z - 2)
    middle_out_left = (z > 1) & (z < Z - 1)

    def valid(j):
        return (j >= 0) & (j < H)

    @pl.loop(0, H + 3 * Z - 5)
    def _(t):
        @pl.when(t < H)
        def _():
            arrive(1, t)
            arrive(2, t)

            @pl.when(t + ahead < H)
            def _():
                for which in (1, 2, 0):
                    fetch(which, t + ahead)

            @pl.when(keys_right)
            def _():
                key_copy(ext.at[t, :, W], t, z, to_right).start()

            @pl.when(has_right)
            def _():
                halo_right(t).start()

            @pl.when(has_left)
            def _():
                halo_left(t).start()

            arrive(0, t)

        @pl.when(valid(t - 1) & is_last)
        def _():
            query_left(t - 1).start()

        @pl.when(valid(t - 1) & has_right & has_left)
        def _():
            halo_left(t - 1).wait_recv()
            key_copy(ext.at[t - 1, :, F + W], t - 1, z + 1, to_left).start()

        for d in range(1, Z - 1):
            @pl.when(valid(t - d) & (z - d >= 0) & keys_right)
            def _():
                key_here(t - d, z - d, to_right).wait_recv()
                key_here(t - d, z - d, to_right).start()

        for d in range(2, Z):
            @pl.when(valid(t - d) & (z + d < Z) & has_left)
            def _():
                key_here(t - d, z + d, to_left).wait_recv()
                key_here(t - d, z + d, to_left).start()

        now = t - delay

        @pl.when(valid(now))
        def _():
            @pl.when(has_left)
            def _():
                halo_right(now).wait_recv()

            @pl.when(is_first)
            def _():
                halo_left(now).wait_recv()
                for g in range(2, Z):
                    key_here(now, g, to_left).wait_recv()

            @pl.when(is_helper)
            def _():
                query_left(now).wait_recv()
                for g in range(Z - 2):
                    key_here(now, g, to_right).wait_recv()

            @pl.when(is_last)
            def _():
                query_left(now).wait_send()

            compute(now)

        jl = t - left_delay

        @pl.when(valid(jl))
        def _():
            @pl.when(is_last)
            def _():
                sum_left_first(jl).start()

            @pl.when(is_helper)
            def _():
                sum_left_first(jl).wait_recv()
                add_raw(lsum, jl, Z - 1)

            @pl.when(middle_in_left)
            def _():
                sum_left_full(jl).wait_recv()
                lsum[jl] = lsum[jl] + coef[jl]

            @pl.when(is_first)
            def _():
                sum_left_last(jl).wait_recv()

            @pl.when(middle_out_left)
            def _():
                sum_left_full(jl).start()

            @pl.when(from_first)
            def _():
                fill_edge(edge_l, lsum, jl, 0)
                sum_left_last(jl).start()

        jr = t - right_delay

        @pl.when(valid(jr))
        def _():
            @pl.when(is_first)
            def _():
                sum_right_first(jr).start()

            @pl.when(from_first)
            def _():
                sum_right_first(jr).wait_recv()
                add_raw(rsum, jr, 0)

            @pl.when(middle_in_right)
            def _():
                sum_right_full(jr).wait_recv()
                rsum[jr] = rsum[jr] + coef[jr]

            @pl.when(is_last)
            def _():
                sum_right_last(jr).wait_recv()

            @pl.when(middle_out_right)
            def _():
                sum_right_full(jr).start()

            @pl.when(is_helper)
            def _():
                fill_edge(edge_r, rsum, jr, Z - 1)
                sum_right_last(jr).start()

        jf = t - last_delay

        @pl.when(valid(jf))
        def _():
            finish(jf)

    @pl.loop(0, H)
    def _(j):
        for which in range(3):
            swap(which, j).wait_send()

        @pl.when(keys_right)
        def _():
            key_copy(ext.at[j, :, W], j, z, to_right).wait_send()

        @pl.when(has_right)
        def _():
            halo_right(j).wait_send()

        @pl.when(has_left)
        def _():
            halo_left(j).wait_send()

        @pl.when(is_first)
        def _():
            sum_right_first(j).wait_send()

        @pl.when(middle_out_right)
        def _():
            sum_right_full(j).wait_send()

        @pl.when(is_helper)
        def _():
            sum_right_last(j).wait_send()

        @pl.when(is_last)
        def _():
            sum_left_first(j).wait_send()

        @pl.when(middle_out_left)
        def _():
            sum_left_full(j).wait_send()

        @pl.when(from_first)
        def _():
            sum_left_last(j).wait_send()

        @pl.when(has_left & has_right)
        def _():
            key_copy(ext.at[j, :, F + W], j, z + 1, to_left).wait_send()

        for d in range(1, Z - 1):
            @pl.when((z - d >= 0) & keys_right)
            def _():
                key_here(j, z - d, to_right).wait_send()

        for d in range(2, Z):
            @pl.when((z + d < Z) & has_left)
            def _():
                key_here(j, z + d, to_left).wait_send()

        out_own(j).wait()

        @pl.when(alone(p, j))
        def _():
            out_other(j).wait_send()

        @pl.when(alone(other, j))
        def _():
            out_other(j).wait_recv()


def basis_table(total_frames, top):
    frames = np.arange(total_frames)
    columns = [np.full(total_frames, math.sqrt(1.0 / total_frames))]
    for k in range(1, top + 1):
        phase = 2.0 * math.pi * ((k * frames) % total_frames) / total_frames
        columns.append(math.sqrt(2.0 / total_frames) * np.cos(phase))
        columns.append(math.sqrt(2.0 / total_frames) * np.sin(phase))
    return np.stack(columns, axis=1).astype(np.float32)


def shards(queries, key_states, value_states, windows, strides, cutoffs):
    F, S, channels = queries.shape
    Z = lax.axis_size("frm")
    heads = channels // DH
    H = (heads + 1) // 2
    SHARED = 2 * H - heads
    W = F // 2
    basis = basis_table(F * Z, F * Z // 8)
    NC = basis.shape[1]
    assert lax.axis_size("pos") == 2 and F == KSTRIDE and Z >= 3 and NC >= F
    TOK = 2 * S
    dma = pltpu.SemaphoreType.DMA
    f32, bf16 = jnp.float32, jnp.bfloat16
    return pl.pallas_call(
        functools.partial(kernel, (F, S, H, SHARED, Z, W, NC)),
        out_shape=jax.ShapeDtypeStruct(queries.shape, f32),
        in_specs=[pl.BlockSpec(memory_space=pltpu.SMEM)] * 4 + [pl.BlockSpec(memory_space=pl.ANY)] * 3,
        out_specs=pl.BlockSpec(memory_space=pl.ANY),
        scratch_shapes=[
            pltpu.VMEM((H, 2, F + 2 * W, TOK, DH), f32),
            pltpu.VMEM((H, 2, Z, TOK, DH), f32),
            pltpu.VMEM((H, 2 * F, TOK, DH), f32),
            pltpu.VMEM((H, NC, TOK, DH), f32),
            pltpu.VMEM((H, NC, TOK, DH), f32),
            pltpu.VMEM((H, NC, TOK, DH), f32),
            pltpu.VMEM((H, F, TOK, DH), f32),
            pltpu.VMEM((H, F, TOK, DH), f32),
            pltpu.VMEM((2 * F, TOK, DH), f32),
            pltpu.VMEM((4 * DH, (F + 2 * W) * TOK), bf16),
            pltpu.VMEM(((F + 2 * W) * TOK, 2 * DH), bf16),
            pltpu.VMEM((4 * DH, Z * TOK), bf16),
            pltpu.VMEM((Z * TOK, 2 * DH), bf16),
            dma((3, H)), dma((3, H)), dma((3, H)),
            dma((H,)), dma((H,)), dma((H,)), dma((H,)),
            dma((H, Z)), dma((H, Z)),
            dma((H,)), dma((H,)), dma((H,)), dma((H,)),
            dma((H,)), dma((H,)), dma((H,)), dma((H,)), dma((H,)),
        ],
        compiler_params=pltpu.CompilerParams(
            collective_id=0, has_side_effects=True, vmem_limit_bytes=60 * 1024 * 1024
        ),
    )(windows, strides, cutoffs, jnp.asarray(basis.reshape(-1)), queries, key_states, value_states)


def solution(mesh):
    in_specs = (
        P(("grp", "frm"), "pos", "head"),
        P(("grp", "frm"), "pos", "head"),
        P(("grp", "frm"), "pos", "head"),
        P("head"),
        P("head"),
        P("head"),
    )
    out_specs = P(("grp", "frm"), "pos", "head")
    return jax.shard_map(shards, mesh=mesh, in_specs=in_specs, out_specs=out_specs, check_vma=False)
```

```python
import functools
import math

import jax
import jax.numpy as jnp
import numpy as np
from jax import lax
from jax.experimental import pallas as pl
from jax.experimental.pallas import tpu as pltpu
from jax.sharding import PartitionSpec as P

DH = 128
KSTRIDE = 4
MESH = pl.DeviceIdType.MESH
NEG = -1e30


def split_two(x):
    high = x.astype(jnp.bfloat16)
    low = (x - high.astype(jnp.float32)).astype(jnp.bfloat16)
    return high, low


def score_rows(q_wide, keys):
    return jnp.dot(q_wide, keys, preferred_element_type=jnp.float32)


def soft(scores, bias):
    scores = scores + bias
    weights = jnp.exp2(scores - jnp.max(scores, axis=1, keepdims=True))
    return weights, jnp.sum(weights, axis=1, keepdims=True)


def weigh(weights, total, values):
    rows = weights.shape[0]
    both = jnp.concatenate(split_two(weights), axis=0)
    wide = jnp.dot(both, values, preferred_element_type=jnp.float32)
    summed = (wide[:rows, :DH] + wide[:rows, DH:]) + (wide[rows:, :DH] + wide[rows:, DH:])
    return summed / total


def fill_split(key, value, keys_wide, values_wide, row, count):
    kh, kl = split_two(key.T)
    vh, vl = split_two(value)
    rows = pl.ds(row, count)
    keys_wide[0:DH, rows] = kh
    keys_wide[DH : 2 * DH, rows] = kh
    keys_wide[2 * DH : 3 * DH, rows] = kl
    keys_wide[3 * DH : 4 * DH, rows] = kl
    values_wide[rows, 0:DH] = vh
    values_wide[rows, DH : 2 * DH] = vl


def kernel(
    sizes,
    win_ref, str_ref, cut_ref, basis_ref, q_ref, k_ref, v_ref, out_ref,
    ext, far, rowbuf, coef, rsum, lsum, edge_r, edge_l, dbuf, ks, vs, kgs, vgs,
    x_own, x_send, x_recv, hr_send, hr_recv, hl_send, hl_recv, k_send, k_recv,
    cr_send, cr_recv, cl_send, cl_recv, q_send, q_recv, o_own, o_send, o_recv,
):
    F, S, H, SHARED, Z, W, NC = sizes
    TOK = 2 * S
    z = lax.axis_index("frm")
    p = lax.axis_index("pos")
    other = 1 - p
    has_right = z < Z - 1
    has_left = z > 0
    right = jnp.minimum(z + 1, Z - 1)
    left = jnp.maximum(z - 1, 0)
    is_first = z == 0
    is_last = z == Z - 1
    is_helper = z == Z - 2
    HH = H // 2

    def keys_right(j):
        return (z < Z - 2) | (is_helper & (j >= HH))

    to_right, to_left, to_other = {"frm": right}, {"frm": left}, {"pos": other}

    def remote(src, dst, send, recv, to):
        return pltpu.make_async_remote_copy(
            src_ref=src, dst_ref=dst, send_sem=send, recv_sem=recv, device_id=to, device_id_type=MESH
        )

    def col(half, j):
        return pl.ds(pl.multiple_of((half * (H - SHARED) + j) * DH, DH), DH)

    my_rows = pl.ds(pl.multiple_of(p * S, S), S)
    other_rows = pl.ds(pl.multiple_of(other * S, S), S)

    def place(which, j, rows):
        if which == 0:
            return rowbuf.at[j, pl.ds(0, F), rows]
        return ext.at[j, which - 1, pl.ds(W, F), rows]

    sources = (q_ref, k_ref, v_ref)

    def own_copy(which, j):
        return pltpu.make_async_copy(
            sources[which].at[:, :, col(p, j)], place(which, j, my_rows), x_own.at[which, j]
        )

    def swap(which, j):
        return remote(
            sources[which].at[:, :, col(other, j)], place(which, j, my_rows),
            x_send.at[which, j], x_recv.at[which, j], to_other,
        )

    def halo_right(j):
        return remote(
            ext.at[j, :, pl.ds(F, W)], ext.at[j, :, pl.ds(0, W)], hr_send.at[j], hr_recv.at[j], to_right
        )

    def halo_left(j):
        return remote(
            ext.at[j, :, pl.ds(W, W)], ext.at[j, :, pl.ds(F + W, W)], hl_send.at[j], hl_recv.at[j], to_left
        )

    def key_copy(src, j, g, to):
        return remote(src, far.at[j, :, g], k_send.at[j, g], k_recv.at[j, g], to)

    def key_here(j, g, to):
        return key_copy(far.at[j, :, g], j, g, to)

    def sum_right_full(j):
        return remote(rsum.at[j], rsum.at[j], cr_send.at[j], cr_recv.at[j], to_right)

    def sum_right_first(j):
        part = rsum.at[j, pl.ds(0, F)]
        return remote(part, part, cr_send.at[j], cr_recv.at[j], to_right)

    def sum_right_last(j):
        return remote(edge_r.at[j], rsum.at[j, pl.ds(0, F)], cr_send.at[j], cr_recv.at[j], to_right)

    def sum_left_full(j):
        return remote(lsum.at[j], lsum.at[j], cl_send.at[j], cl_recv.at[j], to_left)

    def sum_left_first(j):
        part = lsum.at[j, pl.ds(0, F)]
        return remote(part, part, cl_send.at[j], cl_recv.at[j], to_left)

    def sum_left_last(j):
        return remote(edge_l.at[j], lsum.at[j, pl.ds(0, F)], cl_send.at[j], cl_recv.at[j], to_left)

    def query_left(j):
        return remote(
            rowbuf.at[j, pl.ds(0, F)], rowbuf.at[j, pl.ds(F, F)], q_send.at[j], q_recv.at[j], to_left
        )

    def out_own(j):
        return pltpu.make_async_copy(
            rowbuf.at[j, pl.ds(0, F), my_rows], out_ref.at[:, :, col(p, j)], o_own.at[j]
        )

    def out_other(j):
        return remote(
            rowbuf.at[j, pl.ds(0, F), other_rows], out_ref.at[:, :, col(p, j)], o_send.at[j], o_recv.at[j], to_other
        )

    barrier = pltpu.get_barrier_semaphore()
    pl.semaphore_signal(barrier, inc=1, device_id=to_other, device_id_type=MESH)

    @pl.when(has_right)
    def _():
        pl.semaphore_signal(barrier, inc=1, device_id=to_right, device_id_type=MESH)

    @pl.when(has_left)
    def _():
        pl.semaphore_signal(barrier, inc=1, device_id=to_left, device_id_type=MESH)

    pl.semaphore_wait(barrier, 1 + has_right.astype(jnp.int32) + has_left.astype(jnp.int32))

    def alone(half, j):
        if SHARED == 0:
            return j >= 0
        return jnp.where(half == 0, j < H - SHARED, j >= SHARED)

    def fetch(which, j):
        swap(which, j).start()
        own_copy(which, j).start()

    ahead = min(2, H)
    for first in range(ahead):
        for which in (1, 2, 0):
            fetch(which, first)

    def zero_halo(first):
        @pl.loop(0, H)
        def _(j):
            ext[j, :, first : first + W] = jnp.zeros((2, W, TOK, DH), jnp.float32)

    @pl.when(jnp.logical_not(has_left))
    def _():
        zero_halo(0)

    @pl.when(jnp.logical_not(has_right))
    def _():
        zero_halo(F + W)

    def arrive(which, j):
        own_copy(which, j).wait()
        swap(which, j).wait_recv()

    def compute(j):
        head = p * (H - SHARED) + j
        window = win_ref[head]
        stride = str_ref[head]
        for e in range(F + 2 * W):
            fill_split(ext[j, 0, e], ext[j, 1, e], ks, vs, e * TOK, TOK)

        def bias_row(flags):
            return jnp.concatenate(
                [jnp.full((1, TOK), jnp.where(ok, 0.0, NEG), jnp.float32) for ok in flags], axis=1
            )

        def wide_query(i):
            both = rowbuf[j, pl.ds(i, 2)].reshape(2 * TOK, DH)
            qh, ql = split_two(both * (DH**-0.5 * math.log2(math.e)))
            return jnp.concatenate([qh, ql, qh, ql], axis=1)

        def near_pair(i, q_wide):
            span = (2 * W + 1) * TOK
            rows = pl.ds(i * TOK, span + TOK)
            scores = score_rows(q_wide, ks[:, rows])
            parts, totals = [], []
            for u in range(2):
                flags = []
                for off in range(-W, W + 1):
                    frame = z * F + i + u + off
                    flags.append((abs(off) <= window) & (frame >= 0) & (frame < Z * F))
                part = scores[u * TOK : (u + 1) * TOK, u * TOK : u * TOK + span]
                weights, total = soft(part, bias_row(flags))
                empty = jnp.zeros((TOK, TOK), jnp.float32)
                pieces = [weights, empty] if u == 0 else [empty, weights]
                parts.append(jnp.concatenate(pieces, axis=1))
                totals.append(total)
            return weigh(jnp.concatenate(parts, axis=0), jnp.concatenate(totals, axis=0), vs[rows])

        def far_pair(q_wide, far_bias):
            weights, total = soft(score_rows(q_wide, kgs[...]), far_bias)
            return weigh(weights, total, vgs[...])

        def keep_pair(i, local, wide):
            local = local.reshape(2, TOK, DH)
            rowbuf[j, i : i + 2] = local
            dbuf[i : i + 2] = -local if wide is None else wide.reshape(2, TOK, DH) - local

        no_far = is_last & (j < HH)

        @pl.when(jnp.logical_not(no_far))
        def _():
            far[j, :, z] = ext[j, :, W]

            @pl.when(has_right)
            def _():
                far[j, :, z + 1] = ext[j, :, F + W]

            for g in range(Z):
                fill_split(far[j, 0, g], far[j, 1, g], kgs, vgs, g * TOK, TOK)
            far_bias = bias_row([((g * KSTRIDE) & (stride - 1)) == 0 for g in range(Z)])
            for i in range(0, F, 2):
                q_wide = wide_query(i)
                keep_pair(i, near_pair(i, q_wide), far_pair(q_wide, far_bias))

            @pl.when(is_helper & (j < HH))
            def _():
                for i in range(F, 2 * F, 2):
                    wide = far_pair(wide_query(i), far_bias)
                    dbuf[i : i + 2] = wide.reshape(2, TOK, DH)

        @pl.when(no_far)
        def _():
            for i in range(0, F, 2):
                keep_pair(i, near_pair(i, wide_query(i)), None)

        for c in range(NC):
            coef[j, c] = keep_of(j, c) * project([dbuf[i] for i in range(F)], z, c)

        @pl.when(is_helper & (j < HH))
        def _():
            for c in range(NC):
                more = project([dbuf[F + i] for i in range(F)], Z - 1, c)
                coef[j, c] = coef[j, c] + keep_of(j, c) * more

        @pl.when(is_first)
        def _():
            rsum[j, 0:F] = dbuf[0:F]

        @pl.when(is_last)
        def _():
            lsum[j, 0:F] = dbuf[0:F]

    def keep_of(j, c):
        return jnp.where((c + 1) // 2 <= cut_ref[p * (H - SHARED) + j], 1.0, 0.0)

    def project(frames, at, c):
        acc = frames[0] * basis_ref[at * F * NC + c]
        for i in range(1, F):
            acc = acc + frames[i] * basis_ref[(at * F + i) * NC + c]
        return acc

    def expand(start, totals, at, i):
        for c in range(NC):
            part = totals[c] * basis_ref[(at * F + i) * NC + c]
            start = part if start is None else start + part
        return start

    def finish(j):
        def ends(received):
            totals = [coef[j, c] for c in range(NC)]
            for i in range(F):
                rowbuf[j, i] = expand(rowbuf[j, i] + received[j, i], totals, z, i)

        @pl.when(is_first)
        def _():
            ends(lsum)

        @pl.when(is_last)
        def _():
            ends(rsum)

        @pl.when(has_left & has_right)
        def _():
            totals = [(rsum[j, c] - coef[j, c]) + lsum[j, c] for c in range(NC)]
            for i in range(F):
                rowbuf[j, i] = expand(rowbuf[j, i], totals, z, i)

        out_own(j).start()

        @pl.when(alone(p, j))
        def _():
            out_other(j).start()

    def add_raw(sums, j, at):
        raw = [sums[j, i] for i in range(F)]
        for c in range(NC):
            sums[j, c] = coef[j, c] + keep_of(j, c) * project(raw, at, c)

    def fill_edge(edge, sums, j, at):
        totals = [sums[j, c] for c in range(NC)]
        for i in range(F):
            edge[j, i] = expand(None, totals, at, i)

    delay = jnp.where(is_first | is_last | is_helper, Z - 2, jnp.maximum(z, Z - 1 - z))
    right_delay = Z - 2 + 2 * z
    left_delay = jnp.where(is_last, Z - 2, jnp.where(is_first, 2 * Z, 2 * Z - 2 - z))
    last_delay = jnp.maximum(right_delay, left_delay)
    from_first = z == 1
    middle_in_right = (z > 1) & (z < Z - 1)
    middle_in_left = (z > 0) & (z < Z - 2)
    middle_out_right = (z > 0) & (z < Z - 2)
    middle_out_left = (z > 1) & (z < Z - 1)

    def valid(j):
        return (j >= 0) & (j < H)

    @pl.loop(0, H + max(2 * Z, 3 * Z - 4))
    def _(t):
        @pl.when(t < H)
        def _():
            arrive(1, t)
            arrive(2, t)

            @pl.when(t + ahead < H)
            def _():
                for which in (1, 2, 0):
                    fetch(which, t + ahead)

            @pl.when(keys_right(t))
            def _():
                key_copy(ext.at[t, :, W], t, z, to_right).start()

            @pl.when(has_right)
            def _():
                halo_right(t).start()

            @pl.when(has_left)
            def _():
                halo_left(t).start()

            arrive(0, t)

        @pl.when(valid(t - 1) & is_last & (t - 1 < HH))
        def _():
            query_left(t - 1).start()

        @pl.when(valid(t - 1) & has_right & has_left)
        def _():
            halo_left(t - 1).wait_recv()
            key_copy(ext.at[t - 1, :, F + W], t - 1, z + 1, to_left).start()

        for d in range(1, Z - 1):
            @pl.when(valid(t - d) & (z - d >= 0) & keys_right(t - d))
            def _():
                key_here(t - d, z - d, to_right).wait_recv()
                key_here(t - d, z - d, to_right).start()

        for d in range(2, Z):
            @pl.when(valid(t - d) & (z + d < Z) & has_left)
            def _():
                key_here(t - d, z + d, to_left).wait_recv()
                key_here(t - d, z + d, to_left).start()

        now = t - delay

        @pl.when(valid(now))
        def _():
            @pl.when(has_left)
            def _():
                halo_right(now).wait_recv()

            @pl.when(is_first)
            def _():
                halo_left(now).wait_recv()
                for g in range(2, Z):
                    key_here(now, g, to_left).wait_recv()

            @pl.when(is_helper & (now < HH))
            def _():
                query_left(now).wait_recv()
                for g in range(Z - 2):
                    key_here(now, g, to_right).wait_recv()

            @pl.when(is_last & (now < HH))
            def _():
                query_left(now).wait_send()

            @pl.when(is_last & (now >= HH))
            def _():
                for g in range(Z - 1):
                    key_here(now, g, to_right).wait_recv()

            compute(now)

        jr = t - right_delay

        @pl.when(valid(jr))
        def _():
            @pl.when(is_first)
            def _():
                sum_right_first(jr).start()

            @pl.when(from_first)
            def _():
                sum_right_first(jr).wait_recv()
                add_raw(rsum, jr, 0)

            @pl.when(middle_in_right)
            def _():
                sum_right_full(jr).wait_recv()
                rsum[jr] = rsum[jr] + coef[jr]

            @pl.when(is_last)
            def _():
                sum_right_last(jr).wait_recv()

            @pl.when(middle_out_right)
            def _():
                sum_right_full(jr).start()

            @pl.when(is_helper)
            def _():
                fill_edge(edge_r, rsum, jr, Z - 1)
                sum_right_last(jr).start()

        jl = t - left_delay

        @pl.when(valid(jl))
        def _():
            @pl.when(is_last)
            def _():
                sum_left_first(jl).start()

            @pl.when(is_helper)
            def _():
                sum_left_first(jl).wait_recv()
                add_raw(lsum, jl, Z - 1)

            @pl.when(middle_in_left)
            def _():
                sum_left_full(jl).wait_recv()
                lsum[jl] = lsum[jl] + coef[jl]

            @pl.when(is_first)
            def _():
                sum_left_last(jl).wait_recv()

            @pl.when(middle_out_left)
            def _():
                sum_left_full(jl).start()

            @pl.when(from_first)
            def _():
                fill_edge(edge_l, lsum, jl, 0)
                sum_left_last(jl).start()

        jf = t - last_delay

        @pl.when(valid(jf))
        def _():
            finish(jf)

    @pl.loop(0, H)
    def _(j):
        for which in range(3):
            swap(which, j).wait_send()

        @pl.when(keys_right(j))
        def _():
            key_copy(ext.at[j, :, W], j, z, to_right).wait_send()

        @pl.when(has_right)
        def _():
            halo_right(j).wait_send()

        @pl.when(has_left)
        def _():
            halo_left(j).wait_send()

        @pl.when(is_first)
        def _():
            sum_right_first(j).wait_send()

        @pl.when(middle_out_right)
        def _():
            sum_right_full(j).wait_send()

        @pl.when(is_helper)
        def _():
            sum_right_last(j).wait_send()

        @pl.when(is_last)
        def _():
            sum_left_first(j).wait_send()

        @pl.when(middle_out_left)
        def _():
            sum_left_full(j).wait_send()

        @pl.when(from_first)
        def _():
            sum_left_last(j).wait_send()

        @pl.when(has_left & has_right)
        def _():
            key_copy(ext.at[j, :, F + W], j, z + 1, to_left).wait_send()

        for d in range(1, Z - 1):
            @pl.when((z - d >= 0) & keys_right(j))
            def _():
                key_here(j, z - d, to_right).wait_send()

        for d in range(2, Z):
            @pl.when((z + d < Z) & has_left)
            def _():
                key_here(j, z + d, to_left).wait_send()

        out_own(j).wait()

        @pl.when(alone(p, j))
        def _():
            out_other(j).wait_send()

        @pl.when(alone(other, j))
        def _():
            out_other(j).wait_recv()


def basis_table(total_frames, top):
    frames = np.arange(total_frames)
    columns = [np.full(total_frames, math.sqrt(1.0 / total_frames))]
    for k in range(1, top + 1):
        phase = 2.0 * math.pi * ((k * frames) % total_frames) / total_frames
        columns.append(math.sqrt(2.0 / total_frames) * np.cos(phase))
        columns.append(math.sqrt(2.0 / total_frames) * np.sin(phase))
    return np.stack(columns, axis=1).astype(np.float32)


def shards(queries, key_states, value_states, windows, strides, cutoffs):
    F, S, channels = queries.shape
    Z = lax.axis_size("frm")
    heads = channels // DH
    H = (heads + 1) // 2
    SHARED = 2 * H - heads
    W = F // 2
    basis = basis_table(F * Z, F * Z // 8)
    NC = basis.shape[1]
    assert lax.axis_size("pos") == 2 and F == KSTRIDE and Z >= 3 and NC >= F
    TOK = 2 * S
    dma = pltpu.SemaphoreType.DMA
    f32, bf16 = jnp.float32, jnp.bfloat16
    return pl.pallas_call(
        functools.partial(kernel, (F, S, H, SHARED, Z, W, NC)),
        out_shape=jax.ShapeDtypeStruct(queries.shape, f32),
        in_specs=[pl.BlockSpec(memory_space=pltpu.SMEM)] * 4 + [pl.BlockSpec(memory_space=pl.ANY)] * 3,
        out_specs=pl.BlockSpec(memory_space=pl.ANY),
        scratch_shapes=[
            pltpu.VMEM((H, 2, F + 2 * W, TOK, DH), f32),
            pltpu.VMEM((H, 2, Z, TOK, DH), f32),
            pltpu.VMEM((H, 2 * F, TOK, DH), f32),
            pltpu.VMEM((H, NC, TOK, DH), f32),
            pltpu.VMEM((H, NC, TOK, DH), f32),
            pltpu.VMEM((H, NC, TOK, DH), f32),
            pltpu.VMEM((H, F, TOK, DH), f32),
            pltpu.VMEM((H, F, TOK, DH), f32),
            pltpu.VMEM((2 * F, TOK, DH), f32),
            pltpu.VMEM((4 * DH, (F + 2 * W) * TOK), bf16),
            pltpu.VMEM(((F + 2 * W) * TOK, 2 * DH), bf16),
            pltpu.VMEM((4 * DH, Z * TOK), bf16),
            pltpu.VMEM((Z * TOK, 2 * DH), bf16),
            dma((3, H)), dma((3, H)), dma((3, H)),
            dma((H,)), dma((H,)), dma((H,)), dma((H,)),
            dma((H, Z)), dma((H, Z)),
            dma((H,)), dma((H,)), dma((H,)), dma((H,)),
            dma((H,)), dma((H,)), dma((H,)), dma((H,)), dma((H,)),
        ],
        compiler_params=pltpu.CompilerParams(
            collective_id=0, has_side_effects=True, vmem_limit_bytes=60 * 1024 * 1024
        ),
    )(windows, strides, cutoffs, jnp.asarray(basis.reshape(-1)), queries, key_states, value_states)


def solution(mesh):
    in_specs = (
        P(("grp", "frm"), "pos", "head"),
        P(("grp", "frm"), "pos", "head"),
        P(("grp", "frm"), "pos", "head"),
        P("head"),
        P("head"),
        P("head"),
    )
    out_specs = P(("grp", "frm"), "pos", "head")
    return jax.shard_map(shards, mesh=mesh, in_specs=in_specs, out_specs=out_specs, check_vma=False)
```
